256 devices in a mesh: ctx: 128 (over x_lo, y, z, core), head: 2 (over x_hi).
Axes of the slice: x: 4 (x_hi: 2, x_lo: 2; x = x_hi * 2 + x_lo), y: 4, z: 8, core: 2. Of those that a mesh axis runs over, the one named last changes fastest.
Arguments:
- block_order: int32 [256], replicated, may hold values from 0 to 255, as said below
- conv_input: bfloat16 [16384, 2048], P('ctx', 'head'), may hold values from -0.125 to 0.125
- conv_filter: float32 [2048, 128], P('head'), may hold values from -0.5 to 0.5
- query_rows: bfloat16 [16384, 256], P('ctx', 'head'), may hold values from -40 to 40
- key_rows: bfloat16 [16384, 256], P('ctx', 'head'), may hold values from -6 to 6
- value_rows: bfloat16 [16384, 256], P('ctx', 'head'), may hold values from -6 to 6
- out_grad: bfloat16 [16384, 256], P('ctx', 'head'), may hold values from -6 to 6
- qkv_weight: bfloat16 [3, 2048, 256], P(None, None, 'head'), may hold values from -0.21875 to 0.21875
Outputs:
- input_grad: bfloat16 [16384, 2048], P('ctx', 'head')
- filter_grad: float32 [2048, 128], P('head')
The draws below stay inside these ranges and needn't reach their ends.
Inputs may be any that keep to these rules, and one draw needn't show every extreme that they name: `block_order`: A permutation of the 256 blocks of 64 positions; entries 2i and 2i + 1 name the blocks held by index i of ctx, either blocks 2i and 2i + 1 or blocks i and 255 - i, in either order.
All inputs are finite; a program needn't handle non-finite values.
Results may differ from the reference program's by a relative error of at most 0.0064.
Values may be sent and summed in bfloat16 or wider, within the bound.
No kernel may reach another device: no remote copies, remote signals or barrier semaphores. Data moves between devices by JAX's collectives and lax.ppermute only.
A program may use at most 128 MiB of HBM per device.

```python
import jax
import jax.numpy as jnp
from jax import lax

HD = 128
C = 2048
TAPS = 128
HEADS = 2
TOKENS = 16384
BLK = 64
NBLK = 256


def base_keys(key):
    return jax.random.truncated_normal(jax.random.fold_in(key, 13), -3.0, 3.0, (TOKENS, HEADS * HD), jnp.float32)


def draw_key_rows(key, part):
    sample = base_keys(key)
    return sample.astype(jnp.bfloat16)


def draw_query_rows(key, part):
    sample = jax.random.truncated_normal(jax.random.fold_in(key, 14), -3.0, 3.0, (TOKENS, HEADS * HD), jnp.float32)
    return sample.astype(jnp.bfloat16)


def draw_block_order(key, part):
    slot_index = jnp.arange(NBLK, dtype=jnp.int32)
    device_index = slot_index // 2
    swapped = jax.random.randint(jax.random.fold_in(key, 21), (NBLK // 2,), 0, 2)
    inner = jnp.where(swapped[device_index] == 1, 1 - slot_index % 2, slot_index % 2)
    layout = jax.random.randint(jax.random.fold_in(key, 22), (), 0, 2)
    contiguous = 2 * device_index + inner
    mirrored = jnp.where(inner == 0, device_index, NBLK - 1 - device_index)
    return jnp.where(layout == 0, contiguous, mirrored).astype(jnp.int32)


def levels(own_key, extent, cuts, smallest, largest):
    def one(axis_at, shards_of):
        heights = jax.random.uniform(jax.random.fold_in(jax.random.fold_in(own_key, 6), axis_at), (shards_of,), jnp.float32, smallest / len(cuts), largest / len(cuts))
        return jnp.repeat(jnp.exp(heights), extent[axis_at] // shards_of).reshape((-1,) + (1,) * (len(extent) - axis_at - 1))

    factor_of = one(*cuts[0])
    for cut in cuts[1:]:
        factor_of = factor_of * one(*cut)
    return factor_of


def normal_values(rng, shape, scale, bound, pieces=(), kind=jnp.bfloat16):
    result = scale * jax.random.normal(rng, shape, jnp.float32)
    if pieces:
        result = result * levels(rng, shape, pieces, -0.22, 0.18)
    return jnp.clip(result, -bound, bound).astype(kind)


def setup_inputs(seed: int = 0) -> dict:
    splits = jax.random.split(jax.random.key(seed), 9)
    return {
        "block_order": draw_block_order(jax.random.fold_in(splits[8], 71), 0),
        "conv_input": normal_values(splits[1], (TOKENS, C), (TOKENS ** -0.5), 0.125, ((0, 128), (1, 2))),
        "conv_filter": normal_values(splits[2], (C, TAPS), TAPS ** -0.5, 0.5, ((0, 2),), jnp.float32),
        "query_rows": draw_query_rows(jax.random.fold_in(splits[8], 71), 0),
        "key_rows": draw_key_rows(jax.random.fold_in(splits[8], 71), 0),
        "value_rows": normal_values(splits[5], (TOKENS, HEADS * HD), 1.0, 6.0, ((0, 128), (1, 2))),
        "out_grad": normal_values(splits[6], (TOKENS, HEADS * HD), 1.0, 6.0, ((0, 128), (1, 2))),
        "qkv_weight": normal_values(splits[7], (3, C, HEADS * HD), (3 * HEADS * HD) ** -0.5, 0.21875, ((2, 2),)),
    }


LOWEST = -1.0e30


def token_positions(block_order):
    offsets = jnp.arange(BLK, dtype=jnp.int32)
    return (block_order[:, None] * BLK + offsets[None, :]).reshape(-1).astype(jnp.int32)


def head_backward(queries, keys_head, values_head, grads_out, positions):
    softmax_scale = HD ** -0.5
    block_rows = 512 if TOKENS % 512 == 0 else TOKENS
    block_count = TOKENS // block_rows

    def per_query(block_index):
        first_row = (block_index * block_rows).astype(jnp.int32)
        query_piece = lax.dynamic_slice_in_dim(queries, first_row, block_rows, 0)
        grad_piece = lax.dynamic_slice_in_dim(grads_out, first_row, block_rows, 0)
        query_pos = lax.dynamic_slice_in_dim(positions, first_row, block_rows, 0)
        visible = positions[None, :] <= query_pos[:, None]
        scores = jnp.dot(query_piece, keys_head.T, preferred_element_type=jnp.float32) * softmax_scale
        scores = jnp.where(visible, scores, LOWEST)
        row_max = jnp.max(scores, axis=1)
        weights = jnp.where(visible, jnp.exp(scores - row_max[:, None]), 0.0)
        norm_sum = jnp.sum(weights, axis=1)
        dprobs = jnp.dot(grad_piece, values_head.T, preferred_element_type=jnp.float32)
        lse_rows = row_max + jnp.log(norm_sum)
        delta_rows = jnp.sum(weights * dprobs, axis=1) / norm_sum
        soft_probs = jnp.where(visible, jnp.exp(scores - lse_rows[:, None]), 0.0)
        dscores = (soft_probs * (dprobs - delta_rows[:, None])).astype(jnp.bfloat16)
        query_acc = jnp.dot(dscores, keys_head, preferred_element_type=jnp.float32)
        return query_acc, lse_rows, delta_rows

    query_acc, lse_all, delta_all = lax.map(per_query, jnp.arange(block_count, dtype=jnp.int32))
    lse_all = lse_all.reshape(-1)
    delta_all = delta_all.reshape(-1)

    def per_key(block_index):
        first_row = (block_index * block_rows).astype(jnp.int32)
        key_piece = lax.dynamic_slice_in_dim(keys_head, first_row, block_rows, 0)
        value_piece = lax.dynamic_slice_in_dim(values_head, first_row, block_rows, 0)
        key_pos = lax.dynamic_slice_in_dim(positions, first_row, block_rows, 0)
        visible = key_pos[None, :] <= positions[:, None]
        scores = jnp.dot(queries, key_piece.T, preferred_element_type=jnp.float32) * softmax_scale
        soft_probs = jnp.where(visible, jnp.exp(scores - lse_all[:, None]), 0.0)
        dprobs = jnp.dot(grads_out, value_piece.T, preferred_element_type=jnp.float32)
        dscores = (soft_probs * (dprobs - delta_all[:, None])).astype(jnp.bfloat16)
        key_acc = jnp.dot(dscores.T, queries, preferred_element_type=jnp.float32)
        value_acc = jnp.dot(soft_probs.astype(jnp.bfloat16).T, grads_out, preferred_element_type=jnp.float32)
        return key_acc, value_acc

    key_acc, value_acc = lax.map(per_key, jnp.arange(block_count, dtype=jnp.int32))
    query_grad = (softmax_scale * query_acc.reshape(TOKENS, HD)).astype(jnp.bfloat16)
    key_grad = (softmax_scale * key_acc.reshape(TOKENS, HD)).astype(jnp.bfloat16)
    value_grad = value_acc.reshape(TOKENS, HD).astype(jnp.bfloat16)
    return query_grad, key_grad, value_grad


def reference(block_order, conv_input, conv_filter, query_rows, key_rows, value_rows, out_grad, qkv_weight):
    positions = token_positions(block_order)
    head_grads = [[], [], []]
    for head_index in range(HEADS):
        columns = slice(head_index * HD, (head_index + 1) * HD)
        results = head_backward(query_rows[:, columns], key_rows[:, columns], value_rows[:, columns], out_grad[:, columns], positions)
        for which in range(3):
            head_grads[which].append(results[which])
    stacked = [jnp.concatenate(head_grads[which], axis=1) for which in range(3)]
    channel_sum = jnp.dot(stacked[0], qkv_weight[0].T, preferred_element_type=jnp.float32)
    channel_sum = channel_sum + jnp.dot(stacked[1], qkv_weight[1].T, preferred_element_type=jnp.float32)
    channel_sum = channel_sum + jnp.dot(stacked[2], qkv_weight[2].T, preferred_element_type=jnp.float32)
    conv_grad = channel_sum.astype(jnp.bfloat16)
    inverse = jnp.zeros((TOKENS,), jnp.int32).at[positions].set(jnp.arange(TOKENS, dtype=jnp.int32))
    grad_seq = conv_grad[inverse].astype(jnp.float32)
    input_seq = conv_input[inverse].astype(jnp.float32)
    grad_padded = jnp.concatenate((grad_seq, jnp.zeros((TAPS - 1, C), jnp.float32)), axis=0)

    def add_tap(tap_index, running):
        shifted = lax.dynamic_slice_in_dim(grad_padded, tap_index, TOKENS, 0)
        tap_column = lax.dynamic_slice_in_dim(conv_filter, tap_index, 1, 1)
        return running + tap_column[:, 0][None, :] * shifted

    input_seq_grad = lax.fori_loop(0, TAPS, add_tap, jnp.zeros((TOKENS, C), jnp.float32))
    input_padded = jnp.concatenate((jnp.zeros((TAPS - 1, C), jnp.float32), input_seq), axis=0)

    def lag_sum(tap_index):
        shifted = lax.dynamic_slice_in_dim(input_padded, (TAPS - 1 - tap_index).astype(jnp.int32), TOKENS, 0)
        return jnp.sum(grad_seq * shifted, axis=0)

    filter_grad = lax.map(lag_sum, jnp.arange(TAPS, dtype=jnp.int32)).T
    input_grad = input_seq_grad[positions].astype(jnp.bfloat16)
    return input_grad, filter_grad
```

```python
import functools

import jax
import jax.numpy as jnp
from jax import lax
from jax.experimental import pallas as pl
from jax.experimental.pallas import tpu as pltpu
from jax.sharding import Mesh
from jax.sharding import PartitionSpec as P

HD = 128
TAPS = 128
BLK = 64
XL, Y, Z, CORE, HEAD = 2, 4, 8, 2, 2
QSETS = XL * Y
KSETS = Z * CORE
ROWS = 2 * BLK
NQ = KSETS * ROWS
NK = QSETS * ROWS
CTX = ("xl", "y", "z", "core")
LOWEST = -1e30
LOG2E = 1.4426950408889634
SCALE = HD**-0.5
QB = 256
BF = jnp.bfloat16
F32 = jnp.float32
LANES = 128


def nt(a, b):
    return lax.dot_general(a, b, (((1,), (1,)), ((), ())), preferred_element_type=F32)


def tn(a, b):
    return lax.dot_general(a, b, (((0,), (0,)), ((), ())), preferred_element_type=F32)


def nn(a, b):
    return lax.dot_general(a, b, (((1,), (0,)), ((), ())), preferred_element_type=F32)


def scores_t(q, k, kpos, qpos):
    s = nt(k, q) * (SCALE * LOG2E)
    return jnp.where(kpos <= qpos, s, LOWEST)


def stats_kernel(core_ref, q_ref, g_ref, k_ref, v_ref, kpos_ref, qpos_ref, lse_ref, delta_ref):
    s = scores_t(q_ref[...], k_ref[...], kpos_ref[...], qpos_ref[...])
    dp = nt(v_ref[...], g_ref[...])
    top = jnp.max(s, axis=0, keepdims=True)
    w = jnp.exp2(s - top)
    norm = jnp.sum(w, axis=0, keepdims=True)
    cross = jnp.sum(w * dp, axis=0, keepdims=True)
    lse_ref[...] = top + jnp.log2(norm)
    delta_ref[...] = cross / norm


def grads_kernel(
    core_ref, q_ref, g_ref, k_ref, v_ref, kpos_ref, qpos_ref, lse_ref, delta_ref, dq_ref, dkv_ref, dk_acc, dv_acc
):
    step = pl.program_id(0)

    @pl.when(step == 0)
    def _():
        dk_acc[...] = jnp.zeros_like(dk_acc)
        dv_acc[...] = jnp.zeros_like(dv_acc)

    parts = lse_ref[:, 0, :]
    top = jnp.max(parts, axis=0, keepdims=True)
    lse = top + jnp.log2(jnp.sum(jnp.exp2(parts - top), axis=0, keepdims=True))
    delta = jnp.sum(jnp.exp2(parts - lse) * delta_ref[:, 0, :], axis=0, keepdims=True)
    q = q_ref[...]
    g = g_ref[...]
    s = scores_t(q, k_ref[...], kpos_ref[...], qpos_ref[...])
    p = jnp.exp2(s - lse)
    dp = nt(v_ref[...], g)
    ds = (p * (dp - delta)).astype(BF)
    dv_acc[...] += nn(p.astype(BF), g)
    dk_acc[...] += nn(ds, q)
    dq_ref[...] = (SCALE * tn(ds, k_ref[...])).astype(dq_ref.dtype)

    @pl.when(step == pl.num_programs(0) - 1)
    def _():
        dkv_ref[:, :HD] = (SCALE * dk_acc[...]).astype(dkv_ref.dtype)
        dkv_ref[:, HD:] = dv_acc[...].astype(dkv_ref.dtype)


def row_specs():
    half = NQ // 2 // QB
    rows = lambda col: pl.BlockSpec((QB, HD), lambda i, c: (i, col))
    keys = lambda col: pl.BlockSpec((NK, HD), lambda i, c: (0, col))
    ins = [
        rows(0),
        rows(1),
        keys(0),
        keys(1),
        pl.BlockSpec((NK, 1), lambda i, c: (0, 0)),
        pl.BlockSpec((1, QB), lambda i, c: (0, i)),
    ]
    place = lambda i, c: jnp.where(c[0] == 0, i, lax.rem(i + half, 2 * half))
    return ins, place


def attention_stats(core, qg, kv, kpos, qpos):
    ins, place = row_specs()
    stat = pl.BlockSpec((1, QB), lambda i, c: (0, place(i, c)))
    return pl.pallas_call(
        stats_kernel,
        grid_spec=pltpu.PrefetchScalarGridSpec(
            num_scalar_prefetch=1, grid=(NQ // QB,), in_specs=ins, out_specs=[stat, stat]
        ),
        out_shape=[jax.ShapeDtypeStruct((1, NQ), F32)] * 2,
        compiler_params=pltpu.CompilerParams(vmem_limit_bytes=40 << 20),
        name="attention_stats",
    )(core, qg, qg, kv, kv, kpos, qpos)


def attention_grads(core, qg, kv, kpos, qpos, lse_parts, delta_parts):
    ins, place = row_specs()
    stat = pl.BlockSpec((KSETS, 1, QB), lambda i, c: (0, 0, place(i, c)))
    return pl.pallas_call(
        grads_kernel,
        grid_spec=pltpu.PrefetchScalarGridSpec(
            num_scalar_prefetch=1,
            grid=(NQ // QB,),
            in_specs=ins + [stat, stat],
            out_specs=[
                pl.BlockSpec((QB, HD), lambda i, c: (i, 0)),
                pl.BlockSpec((NK, 2 * HD), lambda i, c: (0, 0)),
            ],
            scratch_shapes=[pltpu.VMEM((NK, HD), F32), pltpu.VMEM((NK, HD), F32)],
        ),
        out_shape=[jax.ShapeDtypeStruct((NQ, HD), BF), jax.ShapeDtypeStruct((NK, 2 * HD), BF)],
        compiler_params=pltpu.CompilerParams(vmem_limit_bytes=40 << 20),
        name="attention_grads",
    )(core, qg, qg, kv, kv, kpos, qpos, lse_parts, delta_parts)


def conv_kernel(n_grad, n_in, picks_ref, *refs):
    grads = refs[:n_grad]
    ins = refs[n_grad : n_grad + n_in]
    taps_ref, out_ref, filt_ref, gcand, xcand, gext, xext, lag = refs[n_grad + n_in :]

    def load(cands, stack):
        at = 0
        for ref in cands:
            for b in range(ref.shape[0] // BLK):
                stack[at] = ref[b * BLK : (b + 1) * BLK, :].astype(F32)
                at += 1
        stack[at] = jnp.zeros((BLK, LANES), F32)

    load(grads, gcand)
    load(ins, xcand)
    for slot in range(2):
        for part in range(3):
            gext[slot, part * BLK : (part + 1) * BLK, :] = gcand[picks_ref[slot * 3 + part]]
            xext[slot, part * BLK : (part + 1) * BLK, :] = xcand[picks_ref[6 + slot * 3 + part]]
    for slot in range(2):
        acc = jnp.zeros((BLK, LANES), F32)
        for j in range(TAPS):
            acc = acc + taps_ref[j : j + 1, :] * gext[slot, j : j + BLK, :]
        out_ref[slot * BLK : (slot + 1) * BLK, :] = acc.astype(BF)
    own = [gext[slot, :BLK, :] for slot in range(2)]
    for j in range(TAPS):
        total = None
        for slot in range(2):
            prod = own[slot] * xext[slot, 2 * BLK - j : 3 * BLK - j, :]
            prod = jnp.sum(prod.reshape(BLK // 8, 8, LANES), axis=0)
            total = prod if total is None else total + prod
        lag[j] = total
    filt_ref[0] = jnp.sum(lag[...], axis=1).T


def conv_grads(core, picks, grads, ins, taps):
    channels = taps.shape[1]
    tiles = channels // LANES
    half = tiles // 2
    column = lambda a: pl.BlockSpec((a.shape[0], LANES), lambda i, p: (0, i))
    which = lambda i, p: (jnp.where(i // half == p[12], 0, 1), lax.rem(i, half), 0)
    blocks = lambda arrays: sum(a.shape[0] // BLK for a in arrays) + 1
    return pl.pallas_call(
        functools.partial(conv_kernel, len(grads), len(ins)),
        grid_spec=pltpu.PrefetchScalarGridSpec(
            num_scalar_prefetch=1,
            grid=(tiles,),
            in_specs=[column(a) for a in grads] + [column(a) for a in ins] + [column(taps)],
            out_specs=[
                pl.BlockSpec((ROWS, LANES), lambda i, p: (0, i)),
                pl.BlockSpec((1, LANES, TAPS), which),
            ],
            scratch_shapes=[
                pltpu.VMEM((blocks(grads), BLK, LANES), F32),
                pltpu.VMEM((blocks(ins), BLK, LANES), F32),
                pltpu.VMEM((2, 3 * BLK, LANES), F32),
                pltpu.VMEM((2, 3 * BLK, LANES), F32),
                pltpu.VMEM((TAPS, 8, LANES), F32),
            ],
        ),
        out_shape=[
            jax.ShapeDtypeStruct((ROWS, channels), BF),
            jax.ShapeDtypeStruct((2, channels // 2, TAPS), F32),
        ],
        compiler_params=pltpu.CompilerParams(vmem_limit_bytes=40 << 20),
        name="conv_grads",
    )(jnp.concatenate((picks, core)), *grads, *ins, taps)


def to_all(x, axes, count):
    return lax.all_to_all(jnp.broadcast_to(x[None], (count,) + x.shape), axes, 0, 0, tiled=True)


def swap(x, axis):
    return lax.ppermute(x, axis, [(0, 1), (1, 0)])


def from_ctx(x, distance):
    n = XL * Y * Z * CORE
    return lax.ppermute(x, CTX, [(i + distance, i) for i in range(n) if 0 <= i + distance < n])


def local(block_order, conv_input, conv_filter, query_rows, key_rows, value_rows, out_grad, qkv_weight):
    core = lax.axis_index("core")
    core_arr = core.reshape(1).astype(jnp.int32)
    head = lax.axis_index("head")
    qset = lax.axis_index("xl") * Y + lax.axis_index("y")
    zi = lax.axis_index("z")
    device = (qset * Z + zi) * CORE + core
    channels = conv_input.shape[1]

    order = block_order.reshape(QSETS, Z, CORE, 2)
    mine = lax.dynamic_index_in_dim(order, qset, 0, keepdims=False)
    q_ids = jnp.stack(
        (
            lax.dynamic_index_in_dim(mine, core, 1, keepdims=False),
            lax.dynamic_index_in_dim(mine, 1 - core, 1, keepdims=False),
        )
    ).reshape(-1)
    k_ids = lax.dynamic_slice(order, (0, zi, core, 0), (QSETS, 1, 1, 2)).reshape(-1)
    offsets = jnp.arange(BLK, dtype=jnp.int32)
    qpos = (q_ids[:, None] * BLK + offsets[None, :]).reshape(1, NQ)
    kpos = (k_ids[:, None] * BLK + offsets[None, :]).reshape(NK, 1)

    kv = to_all(jnp.concatenate((key_rows, value_rows), axis=1), ("xl", "y"), QSETS).reshape(NK, 2 * HD)
    qg_own = to_all(jnp.concatenate((query_rows, out_grad), axis=1), "z", Z).reshape(NQ // 2, 2 * HD)
    qg = jnp.concatenate((qg_own, swap(qg_own, "core")), axis=0)

    lse, delta = attention_stats(core_arr, qg, kv, kpos, qpos)
    stats = to_all(jnp.concatenate((lse, delta), axis=0), ("z", "core"), KSETS)
    stats = stats.reshape(KSETS, 2, NQ)
    dq, dkv = attention_grads(core_arr, qg, kv, kpos, qpos, stats[:, :1], stats[:, 1:])

    dq_half = dq[: NQ // 2].astype(F32) + swap(dq[NQ // 2 :], "core").astype(F32)
    dq_parts = lax.all_to_all(dq_half.astype(BF).reshape(Z, ROWS, HD), "z", 0, 0, tiled=True)
    dkv_parts = lax.all_to_all(dkv.reshape(QSETS, ROWS, 2 * HD), ("xl", "y"), 0, 0, tiled=True)
    query_grad = jnp.sum(dq_parts.astype(F32), axis=0).astype(BF)
    kv_grad = jnp.sum(dkv_parts.astype(F32), axis=0).astype(BF)
    grads = jnp.concatenate((query_grad, kv_grad), axis=1)

    w_own = lax.dynamic_slice_in_dim(qkv_weight, head * channels, channels, 1)
    w_other = swap(lax.dynamic_slice_in_dim(qkv_weight, (1 - head) * channels, channels, 1), "head")
    grads_other = swap(grads, "head")
    conv_grad = jnp.zeros((ROWS, channels), F32)
    for which in range(3):
        cols = slice(which * HD, (which + 1) * HD)
        conv_grad = conv_grad + nt(grads[:, cols], w_own[which]) + nt(grads_other[:, cols], w_other[which])
    conv_grad = conv_grad.astype(BF)

    ids = lax.dynamic_slice_in_dim(block_order, device * 2, 2, 0)
    swapped = ids[0] > ids[1]
    blocks_of = lambda a: (a[:BLK], a[BLK:])

    def low_high(a):
        first, second = blocks_of(a)
        return jnp.where(swapped, second, first), jnp.where(swapped, first, second)

    g_low, g_high = low_high(conv_grad)
    x_low, x_high = low_high(conv_input)
    grad_list = [
        conv_grad,
        from_ctx(g_low, 1),
        from_ctx(g_high, 1),
        from_ctx(g_low, 2),
        from_ctx(g_high, -1),
        from_ctx(g_high, -2),
    ]
    in_list = [
        conv_input,
        from_ctx(x_low, -1),
        from_ctx(x_high, -1),
        from_ctx(x_low, -2),
        from_ctx(x_low, 1),
        from_ctx(x_high, 1),
        from_ctx(x_high, 2),
    ]
    padded = jnp.concatenate((jnp.full((4,), -1000, jnp.int32), block_order, jnp.full((4,), -1000, jnp.int32)))
    near = lax.dynamic_slice_in_dim(padded, device * 2, 10, 0).reshape(5, 2)
    low, high = jnp.min(near, axis=1), jnp.max(near, axis=1)
    grad_ids = jnp.stack((ids[0], ids[1], low[3], high[3], low[4], high[1], high[0]))
    in_ids = jnp.stack((ids[0], ids[1], low[1], high[1], low[0], low[3], high[3], high[4]))

    def pick(wanted, have):
        hit = wanted[:, None] == have[None, :]
        return jnp.where(jnp.any(hit, axis=1), jnp.argmax(hit, axis=1), have.shape[0]).astype(jnp.int32)

    steps = jnp.arange(3, dtype=jnp.int32)
    later = (ids[:, None] + steps[None, :]).reshape(-1)
    earlier = (ids[:, None] + steps[None, :] - 2).reshape(-1)
    picks = jnp.concatenate((pick(later, grad_ids), pick(earlier, in_ids)))
    input_grad, filter_part = conv_grads(core_arr, picks, grad_list, in_list, conv_filter.T)

    mine_sum = filter_part[0] + swap(filter_part[1], "core")
    chips = XL * Y * Z
    parts = lax.all_to_all(
        mine_sum.astype(BF).reshape(chips, channels // 2 // chips, TAPS), ("xl", "y", "z"), 0, 0, tiled=True
    )
    total = jnp.sum(parts.astype(F32), axis=0)
    half = to_all(total, ("xl", "y", "z"), chips).reshape(channels // 2, TAPS)
    other = swap(half, "core")
    filter_grad = jnp.concatenate(
        (jnp.where(core == 0, half, other), jnp.where(core == 0, other, half)), axis=0
    )
    return input_grad, filter_grad


def solution(mesh):
    fine = Mesh(mesh.devices.reshape(XL, Y, Z, CORE, HEAD), CTX + ("head",))
    rows = P(CTX, "head")
    return jax.shard_map(
        local,
        mesh=fine,
        in_specs=(P(), rows, P("head", None), rows, rows, rows, rows, P(None, None, "head")),
        out_specs=(rows, P("head", None)),
        check_vma=False,
    )
```

```python
import functools

import jax
import jax.numpy as jnp
from jax import lax
from jax.experimental import pallas as pl
from jax.experimental.pallas import tpu as pltpu
from jax.sharding import Mesh
from jax.sharding import PartitionSpec as P

HD = 128
TAPS = 128
BLK = 64
XL, Y, Z, CORE, HEAD = 2, 4, 8, 2, 2
ROWS = 2 * BLK
NQ = Z * ROWS
NK = XL * Y * CORE * ROWS
CTX = ("xl", "y", "z", "core")
LOWEST = -1e30
LOG2E = 1.4426950408889634
SCALE = HD**-0.5
QB = 256
BF = jnp.bfloat16
F32 = jnp.float32
LANES = 128


def nt(a, b):
    return lax.dot_general(a, b, (((1,), (1,)), ((), ())), preferred_element_type=F32)


def tn(a, b):
    return lax.dot_general(a, b, (((0,), (0,)), ((), ())), preferred_element_type=F32)


def nn(a, b):
    return lax.dot_general(a, b, (((1,), (0,)), ((), ())), preferred_element_type=F32)


def block_of(order_ref, xl, y, z, core, slot):
    return order_ref[(((xl * Y + y) * Z + z) * CORE + core) * 2 + slot]


def fill_key_positions(place_ref, order_ref, kpos):
    row = lax.broadcasted_iota(jnp.int32, (BLK, LANES), 0)
    at = 0
    for c in range(CORE):
        for b in range(Y):
            for a in range(XL):
                xl = lax.rem(place_ref[0] + a, XL)
                y = lax.rem(place_ref[1] + b, Y)
                core = lax.rem(place_ref[3] + c, CORE)
                for slot in range(2):
                    block = block_of(order_ref, xl, y, place_ref[2], core, slot)
                    kpos[at : at + BLK, :] = row + block * BLK
                    at += BLK


def query_positions(place_ref, order_ref, step):
    lane = lax.broadcasted_iota(jnp.int32, (1, QB), 1)
    pos = jnp.zeros((1, QB), jnp.int32)
    for b in range(QB // BLK):
        at = step * (QB // BLK) + b
        block = block_of(order_ref, place_ref[0], place_ref[1], at // 2, place_ref[3], at % 2)
        pos = jnp.where(lane // BLK == b, block * BLK + lane % BLK, pos)
    return pos


def scores_t(q, k, kpos, qpos):
    s = nt(k, q) * (SCALE * LOG2E)
    seen = jnp.concatenate([kpos[...]] * (QB // LANES), axis=1) <= qpos
    return jnp.where(seen, s, LOWEST)


def stats_kernel(place_ref, order_ref, q_ref, g_ref, k_ref, v_ref, stat_ref, kpos):
    step = pl.program_id(0)

    @pl.when(step == 0)
    def _():
        fill_key_positions(place_ref, order_ref, kpos)

    s = scores_t(q_ref[...], k_ref[...], kpos, query_positions(place_ref, order_ref, step))
    dp = nt(v_ref[...], g_ref[...])
    top = jnp.max(s, axis=0, keepdims=True)
    w = jnp.exp2(s - top)
    norm = jnp.sum(w, axis=0, keepdims=True)
    cross = jnp.sum(w * dp, axis=0, keepdims=True)
    stat = jnp.concatenate((top + jnp.log2(norm), cross / norm), axis=0)
    stat_ref[...] = jnp.broadcast_to(stat[None], stat_ref.shape)


def grads_kernel(
    place_ref, order_ref, q_ref, g_ref, k_ref, v_ref, stat_ref, dq_ref, own_ref, other_ref, dk_acc, dv_acc, kpos
):
    step = pl.program_id(0)

    @pl.when(step == 0)
    def _():
        fill_key_positions(place_ref, order_ref, kpos)
        dk_acc[...] = jnp.zeros_like(dk_acc)
        dv_acc[...] = jnp.zeros_like(dv_acc)

    parts = stat_ref[:, 0, :]
    top = jnp.max(parts, axis=0, keepdims=True)
    lse = top + jnp.log2(jnp.sum(jnp.exp2(parts - top), axis=0, keepdims=True))
    delta = jnp.sum(jnp.exp2(parts - lse) * stat_ref[:, 1, :], axis=0, keepdims=True)
    q = q_ref[...]
    g = g_ref[...]
    s = scores_t(q, k_ref[...], kpos, query_positions(place_ref, order_ref, step))
    p = jnp.exp2(s - lse)
    dp = nt(v_ref[...], g)
    ds = (p * (dp - delta)).astype(BF)
    dv_acc[...] += nn(p.astype(BF), g)
    dk_acc[...] += nn(ds, q)
    dq_ref[...] = (SCALE * tn(ds, k_ref[...])).astype(dq_ref.dtype)

    @pl.when(step == pl.num_programs(0) - 1)
    def _():
        for at, ref in ((0, own_ref), (NK // 2, other_ref)):
            for b in range(Y):
                for a in range(XL):
                    owner = lax.rem(place_ref[0] + a, XL) * Y + lax.rem(place_ref[1] + b, Y)
                    here = pl.ds(at + (b * XL + a) * ROWS, ROWS)
                    there = pl.ds(pl.multiple_of(owner * ROWS, ROWS), ROWS)
                    ref[there, :HD] = SCALE * dk_acc[here, :]
                    ref[there, HD:] = dv_acc[here, :]


def attention_specs():
    rows = lambda col: pl.BlockSpec((QB, HD), lambda i, *_: (i, col))
    keys = lambda col: pl.BlockSpec((NK, HD), lambda i, *_: (0, col))
    return [
        rows(0),
        rows(1),
        keys(0),
        keys(1),
    ]


STAT = pl.BlockSpec((Z, 2, QB), lambda i, *_: (0, 0, i))


def attention_stats(place, order, qg, kv):
    return pl.pallas_call(
        stats_kernel,
        grid_spec=pltpu.PrefetchScalarGridSpec(
            num_scalar_prefetch=2,
            grid=(NQ // QB,),
            in_specs=attention_specs(),
            out_specs=STAT,
            scratch_shapes=[pltpu.VMEM((NK, LANES), jnp.int32)],
        ),
        out_shape=jax.ShapeDtypeStruct((Z, 2, NQ), F32),
        compiler_params=pltpu.CompilerParams(vmem_limit_bytes=40 << 20),
        cost_estimate=pl.CostEstimate(flops=4 * NQ * NK * HD, bytes_accessed=4 << 20, transcendentals=NQ * NK),
        name="attention_stats",
    )(place, order, qg, qg, kv, kv)


def attention_grads(place, order, qg, kv, stats):
    half = pl.BlockSpec((NK // 2, 2 * HD), lambda i, *_: (0, 0))
    return pl.pallas_call(
        grads_kernel,
        grid_spec=pltpu.PrefetchScalarGridSpec(
            num_scalar_prefetch=2,
            grid=(NQ // QB,),
            in_specs=attention_specs() + [STAT],
            out_specs=[pl.BlockSpec((QB, HD), lambda i, *_: (i, 0)), half, half],
            scratch_shapes=[
                pltpu.VMEM((NK, HD), F32),
                pltpu.VMEM((NK, HD), F32),
                pltpu.VMEM((NK, LANES), jnp.int32),
            ],
        ),
        out_shape=[
            jax.ShapeDtypeStruct((NQ, HD), BF),
            jax.ShapeDtypeStruct((NK // 2, 2 * HD), F32),
            jax.ShapeDtypeStruct((NK // 2, 2 * HD), F32),
        ],
        compiler_params=pltpu.CompilerParams(vmem_limit_bytes=40 << 20),
        cost_estimate=pl.CostEstimate(flops=10 * NQ * NK * HD, bytes_accessed=4 << 20, transcendentals=NQ * NK),
        name="attention_grads",
    )(place, order, qg, qg, kv, kv, stats)


def pack_kernel(q_ref, g_ref, k_ref, v_ref, qg_ref, kv_ref):
    kv_ref[:, :HD] = k_ref[...]
    kv_ref[:, HD:] = v_ref[...]
    for i in range(Z):
        qg_ref[i, :, :HD] = q_ref[...]
        qg_ref[i, :, HD:] = g_ref[...]


def pack(q, g, k, v):
    return pl.pallas_call(
        pack_kernel,
        out_shape=[jax.ShapeDtypeStruct((Z, ROWS, 2 * HD), BF), jax.ShapeDtypeStruct((ROWS, 2 * HD), BF)],
        name="pack",
    )(q, g, k, v)


def stack_blocks(refs, stack):
    at = 0
    for ref in refs:
        for b in range(ref.shape[0] // BLK):
            stack[at] = ref[b * BLK : (b + 1) * BLK, :].astype(F32)
            at += 1
    stack[at] = jnp.zeros((BLK, LANES), F32)


def low_high(place_ref, order_ref, distance):
    at = ((place_ref[0] * Y + place_ref[1]) * Z + place_ref[2]) * CORE + place_ref[3] + distance
    inside = jnp.logical_and(at >= 0, at < XL * Y * Z * CORE)
    at = jnp.where(inside, at, 0)
    first, second = order_ref[2 * at], order_ref[2 * at + 1]
    low = jnp.where(inside, jnp.minimum(first, second), -1000)
    high = jnp.where(inside, jnp.maximum(first, second), -1000)
    return low, high


def extend(place_ref, order_ref, have, shift, cand, ext):
    at = ((place_ref[0] * Y + place_ref[1]) * Z + place_ref[2]) * CORE + place_ref[3]
    for slot in range(2):
        own = order_ref[2 * at + slot]
        for part in range(3):
            place = jnp.int32(len(have))
            for i, block in enumerate(have):
                place = jnp.where(block == own + (part + shift), i, place)
            ext[slot, part * BLK : (part + 1) * BLK, :] = cand[place]


def filter_kernel(
    n_in, place_ref, order_ref, q_own, kv_own, q_other, kv_other, w_own, w_other, *refs
):
    ins = refs[:n_in]
    pair_ref, low_ref, high_ref, filt_ref, cand, grad, ext, lag = refs[n_in:]
    cg = jnp.zeros((ROWS, LANES), F32)
    for q_ref, kv_ref, w_ref in ((q_own, kv_own, w_own), (q_other, kv_other, w_other)):
        cg = cg + nt(q_ref[...], w_ref[0])
        cg = cg + nt(kv_ref[:, :HD], w_ref[1])
        cg = cg + nt(kv_ref[:, HD:], w_ref[2])
    grad[...] = cg.astype(BF).astype(F32)
    device = ((place_ref[0] * Y + place_ref[1]) * Z + place_ref[2]) * CORE + place_ref[3]
    first, second = order_ref[2 * device], order_ref[2 * device + 1]
    swapped = (first > second).astype(jnp.int32)
    low = grad[pl.ds(pl.multiple_of(swapped * BLK, BLK), BLK), :].astype(BF)
    high = grad[pl.ds(pl.multiple_of((1 - swapped) * BLK, BLK), BLK), :].astype(BF)
    low_ref[...] = low
    high_ref[...] = high
    pair_ref[:BLK, :] = low
    pair_ref[BLK:, :] = high
    stack_blocks(ins, cand)
    near = [low_high(place_ref, order_ref, d) for d in (-2, -1, 1, 2)]
    device_of = lambda d: 2 * jnp.clip(device + d, 0, XL * Y * Z * CORE - 1)
    inside = lambda d, block: jnp.where(
        jnp.logical_and(device + d >= 0, device + d < XL * Y * Z * CORE), block, -1000
    )
    have = [first, second, near[0][0]]
    have += [inside(-1, order_ref[device_of(-1) + s]) for s in range(2)]
    have += [inside(1, order_ref[device_of(1) + s]) for s in range(2)]
    have += [near[3][1]]
    extend(place_ref, order_ref, have, -2, cand, ext)
    for r in range(8):
        for slot in range(2):
            rows = [grad[slot * BLK + 8 * m : slot * BLK + 8 * m + 8, :] for m in range(BLK // 8)]
            last = 2 * BLK - r
            shifted = [ext[slot, last - TAPS + 8 + 8 * n : last - TAPS + 16 + 8 * n, :] for n in range(23)]
            for a in range(TAPS // 8):
                total = rows[0] * shifted[15 - a]
                for m in range(1, BLK // 8):
                    total = total + rows[m] * shifted[15 - a + m]
                j = 8 * a + r
                lag[j] = total if slot == 0 else lag[j] + total
    filt_ref[0] = jnp.sum(lag[...], axis=1).T


def project_and_filter(place, order, q_own, kv_own, q_other, kv_other, weight, w_other, ins):
    channels = ins[0].shape[1]
    tiles = channels // LANES
    half = tiles // 2
    whole = lambda a: pl.BlockSpec(a.shape, lambda i, p, o: (0, 0))
    column = lambda a: pl.BlockSpec((a.shape[0], LANES), lambda i, p, o: (0, i))
    which = lambda i, p, o: (jnp.where(i // half == p[3], 0, 1), lax.rem(i, half), 0)
    block = lambda rows: pl.BlockSpec((rows, LANES), lambda i, p, o: (0, i))
    blocks = sum(a.shape[0] // BLK for a in ins) + 1
    return pl.pallas_call(
        functools.partial(filter_kernel, len(ins)),
        grid_spec=pltpu.PrefetchScalarGridSpec(
            num_scalar_prefetch=2,
            grid=(tiles,),
            in_specs=[whole(a) for a in (q_own, kv_own, q_other, kv_other)]
            + [
                pl.BlockSpec((3, LANES, HD), lambda i, p, o: (0, p[4] * tiles + i, 0)),
                pl.BlockSpec((3, LANES, HD), lambda i, p, o: (0, i, 0)),
            ]
            + [column(a) for a in ins],
            out_specs=[block(ROWS), block(BLK), block(BLK), pl.BlockSpec((1, LANES, TAPS), which)],
            scratch_shapes=[
                pltpu.VMEM((blocks, BLK, LANES), F32),
                pltpu.VMEM((ROWS, LANES), F32),
                pltpu.VMEM((2, 3 * BLK, LANES), F32),
                pltpu.VMEM((TAPS, 8, LANES), F32),
            ],
        ),
        out_shape=[
            jax.ShapeDtypeStruct((ROWS, channels), BF),
            jax.ShapeDtypeStruct((BLK, channels), BF),
            jax.ShapeDtypeStruct((BLK, channels), BF),
            jax.ShapeDtypeStruct((2, channels // 2, TAPS), F32),
        ],
        compiler_params=pltpu.CompilerParams(vmem_limit_bytes=40 << 20),
        cost_estimate=pl.CostEstimate(flops=4 << 30, bytes_accessed=8 << 20, transcendentals=0),
        name="project_and_filter",
    )(place, order, q_own, kv_own, q_other, kv_other, weight, w_other, *ins)


def conv_kernel(n_grad, place_ref, order_ref, *refs):
    grads = refs[:n_grad]
    filter_ref, out_ref, cand, ext, taps_ref = refs[n_grad:]
    taps_ref[...] = filter_ref[...].T
    stack_blocks(grads, cand)
    near = [low_high(place_ref, order_ref, d) for d in (0, 1, 2, -1, -2)]
    have = [near[0][0], near[0][1], near[1][0], near[1][1], near[2][0], near[3][1], near[4][1]]
    extend(place_ref, order_ref, have, 0, cand, ext)
    for slot in range(2):
        acc = [jnp.zeros((8, LANES), F32) for _ in range(BLK // 8)]
        for r in range(8):
            shifted = [ext[slot, r + 8 * n : r + 8 * n + 8, :] for n in range(23)]
            for a in range(TAPS // 8):
                tap = taps_ref[8 * a + r : 8 * a + r + 1, :]
                for m in range(BLK // 8):
                    acc[m] = acc[m] + tap * shifted[m + a]
        out_ref[slot * BLK : (slot + 1) * BLK, :] = jnp.concatenate(acc, axis=0).astype(BF)


def input_conv(place, order, grads, taps):
    channels = taps.shape[0]
    column = lambda a: pl.BlockSpec((a.shape[0], LANES), lambda i, p, o: (0, i))
    blocks = sum(a.shape[0] // BLK for a in grads) + 1
    return pl.pallas_call(
        functools.partial(conv_kernel, len(grads)),
        grid_spec=pltpu.PrefetchScalarGridSpec(
            num_scalar_prefetch=2,
            grid=(channels // LANES,),
            in_specs=[column(a) for a in grads] + [pl.BlockSpec((LANES, TAPS), lambda i, p, o: (i, 0))],
            out_specs=pl.BlockSpec((ROWS, LANES), lambda i, p, o: (0, i)),
            scratch_shapes=[
                pltpu.VMEM((blocks, BLK, LANES), F32),
                pltpu.VMEM((2, 3 * BLK, LANES), F32),
                pltpu.VMEM((TAPS, LANES), F32),
            ],
        ),
        out_shape=jax.ShapeDtypeStruct((ROWS, channels), BF),
        compiler_params=pltpu.CompilerParams(vmem_limit_bytes=40 << 20),
        cost_estimate=pl.CostEstimate(flops=1 << 20, bytes_accessed=1 << 20, transcendentals=0),
        name="input_conv",
    )(place, order, *grads, taps)


def to_all(x, axes, count):
    return lax.all_to_all(jnp.broadcast_to(x[None], (count,) + x.shape), axes, 0, 0, tiled=True)


def swap(x, axis):
    return lax.ppermute(x, axis, [(0, 1), (1, 0)])


def from_ctx(x, distance):
    n = XL * Y * Z * CORE
    return lax.ppermute(x, CTX, [(i + distance, i) for i in range(n) if 0 <= i + distance < n])


def around(x, step, size, axis):
    return lax.ppermute(x, axis, [((i + step) % size, i) for i in range(size)])


def local(block_order, conv_input, conv_filter, query_rows, key_rows, value_rows, out_grad, qkv_weight):
    coords = [lax.axis_index(axis) for axis in CTX + ("head",)]
    core, head = coords[3], coords[4]
    channels = conv_input.shape[1]
    chips = XL * Y * Z
    entry = lax.iota(jnp.int32, 8)
    place = jnp.zeros((8,), jnp.int32)
    for i, coord in enumerate(coords):
        place = jnp.where(entry == i, coord, place)

    qg, kv = pack(query_rows, out_grad, key_rows, value_rows)
    qg = lax.all_to_all(qg, "z", 0, 0, tiled=True).reshape(NQ, 2 * HD)
    kv_xl = swap(kv, "xl")
    kv = jnp.concatenate((kv, kv_xl), axis=0)
    kv = jnp.concatenate([kv] + [around(kv, s, Y, "y") for s in range(1, Y)], axis=0)
    kv = jnp.concatenate((kv, swap(kv, "core")), axis=0)

    device = ((coords[0] * Y + coords[1]) * Z + coords[2]) * CORE + core
    ids = lax.dynamic_slice_in_dim(block_order, device * 2, 2, 0)
    swapped = (ids[0] > ids[1]).astype(jnp.int32)
    x_low = lax.dynamic_slice_in_dim(conv_input, swapped * BLK, BLK, 0)
    x_high = lax.dynamic_slice_in_dim(conv_input, (1 - swapped) * BLK, BLK, 0)
    w_sent = lax.dynamic_slice_in_dim(qkv_weight, (1 - head) * channels, channels, 1)
    w_sent, x_low, x_high, kv_xl = lax.optimization_barrier((w_sent, x_low, x_high, kv_xl))
    w_other = swap(w_sent, "head")

    stats = attention_stats(place, block_order, qg, kv)
    stats = lax.all_to_all(stats, "z", 0, 0, tiled=True)
    stats, w_other = lax.optimization_barrier((stats, w_other))
    dq, dkv_own, dkv_other = attention_grads(place, block_order, qg, kv, stats)

    dq, x_low, x_high = lax.optimization_barrier((dq, x_low, x_high))
    moved_far = [from_ctx(x_low, -2), from_ctx(x_high, 2)]
    dq_parts = lax.all_to_all(dq.reshape(Z, ROWS, HD), "z", 0, 0, tiled=True)
    dkv = (dkv_own + swap(dkv_other, "core")).astype(BF).reshape(XL * Y, ROWS, 2 * HD)
    dq_parts, dkv, x_near, moved_far = lax.optimization_barrier((dq_parts, dkv, conv_input, moved_far))
    dkv_parts = lax.all_to_all(dkv, ("xl", "y"), 0, 0, tiled=True)
    moved_near = [from_ctx(x_near, -1), from_ctx(x_near, 1)]
    dkv_parts, moved_near = lax.optimization_barrier((dkv_parts, moved_near))
    query_grad = jnp.sum(dq_parts.astype(F32), axis=0).astype(BF)
    q_other = swap(query_grad, "head")
    kv_grad = jnp.sum(dkv_parts.astype(F32), axis=0).astype(BF)
    kv_other = swap(kv_grad, "head")

    ins = [conv_input, moved_far[0], *moved_near, moved_far[1]]
    g_pair, g_low, g_high, filter_part = project_and_filter(
        place, block_order, query_grad, kv_grad, q_other, kv_other, qkv_weight, w_other, ins
    )

    mine_sum = filter_part[0] + swap(filter_part[1], "core")
    far = [from_ctx(g_low, 2), from_ctx(g_high, -2)]
    parts = lax.all_to_all(
        mine_sum.reshape(chips, channels // 2 // chips, TAPS), ("xl", "y", "z"), 0, 0, tiled=True
    )
    parts, far, g_pair, g_high = lax.optimization_barrier((parts, far, g_pair, g_high))
    total = jnp.sum(parts, axis=0)
    total, g_pair, g_high = lax.optimization_barrier((total, g_pair, g_high))
    grads = [g_pair, from_ctx(g_pair, 1), far[0], from_ctx(g_high, -1), far[1]]
    half = to_all(total, ("xl", "y", "z"), chips)
    input_grad = input_conv(place, block_order, grads, conv_filter)
    half, input_grad = lax.optimization_barrier((half, input_grad))
    half = half.reshape(channels // 2, TAPS)
    other = swap(half, "core")
    filter_grad = jnp.concatenate(
        (jnp.where(core == 0, half, other), jnp.where(core == 0, other, half)), axis=0
    )
    return input_grad, filter_grad


def solution(mesh):
    fine = Mesh(mesh.devices.reshape(XL, Y, Z, CORE, HEAD), CTX + ("head",))
    rows = P(CTX, "head")
    return jax.shard_map(
        local,
        mesh=fine,
        in_specs=(P(), rows, P("head", None), rows, rows, rows, rows, P(None, None, "head")),
        out_specs=(rows, P("head", None)),
        check_vma=False,
    )
```

```python
import functools

import jax
import jax.numpy as jnp
from jax import lax
from jax.experimental import pallas as pl
from jax.experimental.pallas import tpu as pltpu
from jax.sharding import Mesh
from jax.sharding import PartitionSpec as P

HD = 128
TAPS = 128
BLK = 64
XL, Y, Z, CORE, HEAD = 2, 4, 8, 2, 2
ROWS = 2 * BLK
NQ = Z * ROWS
NK = XL * Y * CORE * ROWS
CTX = ("xl", "y", "z", "core")
LOWEST = -1e30
LOG2E = 1.4426950408889634
SCALE = HD**-0.5
QB = 256
BF = jnp.bfloat16
F32 = jnp.float32
LANES = 128


def nt(a, b):
    return lax.dot_general(a, b, (((1,), (1,)), ((), ())), preferred_element_type=F32)


def tn(a, b):
    return lax.dot_general(a, b, (((0,), (0,)), ((), ())), preferred_element_type=F32)


def nn(a, b):
    return lax.dot_general(a, b, (((1,), (0,)), ((), ())), preferred_element_type=F32)


def block_of(order_ref, xl, y, z, core, slot):
    return order_ref[(((xl * Y + y) * Z + z) * CORE + core) * 2 + slot]


def fill_key_positions(place_ref, order_ref, kpos):
    row = lax.broadcasted_iota(jnp.int32, (BLK, LANES), 0)
    at = 0
    for c in range(CORE):
        for b in range(Y):
            for a in range(XL):
                xl = lax.rem(place_ref[0] + a, XL)
                y = lax.rem(place_ref[1] + b, Y)
                core = lax.rem(place_ref[3] + c, CORE)
                for slot in range(2):
                    block = block_of(order_ref, xl, y, place_ref[2], core, slot)
                    kpos[at : at + BLK, :] = row + block * BLK
                    at += BLK


def query_positions(place_ref, order_ref, step):
    lane = lax.broadcasted_iota(jnp.int32, (1, QB), 1)
    pos = jnp.zeros((1, QB), jnp.int32)
    for b in range(QB // BLK):
        at = step * (QB // BLK) + b
        block = block_of(order_ref, place_ref[0], place_ref[1], at // 2, place_ref[3], at % 2)
        pos = jnp.where(lane // BLK == b, block * BLK + lane % BLK, pos)
    return pos


def scores_t(q, k, kpos, qpos):
    s = nt(k, q) * (SCALE * LOG2E)
    seen = jnp.concatenate([kpos[...]] * (QB // LANES), axis=1) <= qpos
    return jnp.where(seen, s, LOWEST)


def stats_kernel(place_ref, order_ref, q_ref, g_ref, k_ref, v_ref, stat_ref, kpos):
    step = pl.program_id(0)

    @pl.when(step == 0)
    def _():
        fill_key_positions(place_ref, order_ref, kpos)

    s = scores_t(q_ref[...], k_ref[...], kpos, query_positions(place_ref, order_ref, step))
    dp = nt(v_ref[...], g_ref[...])
    top = jnp.max(s, axis=0, keepdims=True)
    w = jnp.exp2(s - top)
    norm = jnp.sum(w, axis=0, keepdims=True)
    cross = jnp.sum(w * dp, axis=0, keepdims=True)
    stat = jnp.concatenate((top + jnp.log2(norm), cross / norm), axis=0)
    stat_ref[...] = jnp.broadcast_to(stat[None], stat_ref.shape)


def grads_kernel(
    place_ref, order_ref, q_ref, g_ref, k_ref, v_ref, stat_ref, dq_ref, own_ref, other_ref, dk_acc, dv_acc, kpos
):
    step = pl.program_id(0)

    @pl.when(step == 0)
    def _():
        fill_key_positions(place_ref, order_ref, kpos)
        dk_acc[...] = jnp.zeros_like(dk_acc)
        dv_acc[...] = jnp.zeros_like(dv_acc)

    parts = stat_ref[:, 0, :]
    top = jnp.max(parts, axis=0, keepdims=True)
    lse = top + jnp.log2(jnp.sum(jnp.exp2(parts - top), axis=0, keepdims=True))
    delta = jnp.sum(jnp.exp2(parts - lse) * stat_ref[:, 1, :], axis=0, keepdims=True)
    q = q_ref[...]
    g = g_ref[...]
    s = scores_t(q, k_ref[...], kpos, query_positions(place_ref, order_ref, step))
    p = jnp.exp2(s - lse)
    dp = nt(v_ref[...], g)
    ds = (p * (dp - delta)).astype(BF)
    dv_acc[...] += nn(p.astype(BF), g)
    dk_acc[...] += nn(ds, q)
    dq_ref[...] = (SCALE * tn(ds, k_ref[...])).astype(dq_ref.dtype)

    @pl.when(step == pl.num_programs(0) - 1)
    def _():
        for at, ref in ((0, own_ref), (NK // 2, other_ref)):
            for b in range(Y):
                for a in range(XL):
                    owner = lax.rem(place_ref[0] + a, XL) * Y + lax.rem(place_ref[1] + b, Y)
                    here = pl.ds(at + (b * XL + a) * ROWS, ROWS)
                    there = pl.ds(pl.multiple_of(owner * ROWS, ROWS), ROWS)
                    ref[there, :HD] = SCALE * dk_acc[here, :]
                    ref[there, HD:] = dv_acc[here, :]


def attention_specs():
    rows = lambda col: pl.BlockSpec((QB, HD), lambda i, *_: (i, col))
    keys = lambda col: pl.BlockSpec((NK, HD), lambda i, *_: (0, col))
    return [
        rows(0),
        rows(1),
        keys(0),
        keys(1),
    ]


STAT = pl.BlockSpec((Z, 2, QB), lambda i, *_: (0, 0, i))


def attention_stats(place, order, qg, kv):
    return pl.pallas_call(
        stats_kernel,
        grid_spec=pltpu.PrefetchScalarGridSpec(
            num_scalar_prefetch=2,
            grid=(NQ // QB,),
            in_specs=attention_specs(),
            out_specs=STAT,
            scratch_shapes=[pltpu.VMEM((NK, LANES), jnp.int32)],
        ),
        out_shape=jax.ShapeDtypeStruct((Z, 2, NQ), F32),
        compiler_params=pltpu.CompilerParams(vmem_limit_bytes=40 << 20),
        cost_estimate=pl.CostEstimate(flops=4 * NQ * NK * HD, bytes_accessed=4 << 20, transcendentals=NQ * NK),
        name="attention_stats",
    )(place, order, qg, qg, kv, kv)


def attention_grads(place, order, qg, kv, stats):
    half = pl.BlockSpec((NK // 2, 2 * HD), lambda i, *_: (0, 0))
    return pl.pallas_call(
        grads_kernel,
        grid_spec=pltpu.PrefetchScalarGridSpec(
            num_scalar_prefetch=2,
            grid=(NQ // QB,),
            in_specs=attention_specs() + [STAT],
            out_specs=[pl.BlockSpec((QB, HD), lambda i, *_: (i, 0)), half, half],
            scratch_shapes=[
                pltpu.VMEM((NK, HD), F32),
                pltpu.VMEM((NK, HD), F32),
                pltpu.VMEM((NK, LANES), jnp.int32),
            ],
        ),
        out_shape=[
            jax.ShapeDtypeStruct((NQ, HD), BF),
            jax.ShapeDtypeStruct((NK // 2, 2 * HD), F32),
            jax.ShapeDtypeStruct((NK // 2, 2 * HD), F32),
        ],
        compiler_params=pltpu.CompilerParams(vmem_limit_bytes=40 << 20),
        cost_estimate=pl.CostEstimate(flops=10 * NQ * NK * HD, bytes_accessed=4 << 20, transcendentals=NQ * NK),
        name="attention_grads",
    )(place, order, qg, qg, kv, kv, stats)


def pack_kernel(q_ref, g_ref, k_ref, v_ref, qg_ref, kv_ref):
    kv_ref[:, :HD] = k_ref[...]
    kv_ref[:, HD:] = v_ref[...]
    for i in range(Z):
        qg_ref[i, :, :HD] = q_ref[...]
        qg_ref[i, :, HD:] = g_ref[...]


def pack(q, g, k, v):
    return pl.pallas_call(
        pack_kernel,
        out_shape=[jax.ShapeDtypeStruct((Z, ROWS, 2 * HD), BF), jax.ShapeDtypeStruct((ROWS, 2 * HD), BF)],
        name="pack",
    )(q, g, k, v)


def stack_blocks(refs, stack):
    at = 0
    for ref in refs:
        for b in range(ref.shape[0] // BLK):
            stack[at] = ref[b * BLK : (b + 1) * BLK, :].astype(F32)
            at += 1
    stack[at] = jnp.zeros((BLK, LANES), F32)


def device_at(place_ref):
    return ((place_ref[0] * Y + place_ref[1]) * Z + place_ref[2]) * CORE + place_ref[3]


def blocks_at(order_ref, at):
    inside = jnp.logical_and(at >= 0, at < XL * Y * Z * CORE)
    at = jnp.where(inside, at, 0)
    return [jnp.where(inside, order_ref[2 * at + slot], -1000) for slot in range(2)]


def low_high(order_ref, at):
    first, second = blocks_at(order_ref, at)
    return [jnp.minimum(first, second), jnp.maximum(first, second)]


def extend(place_ref, order_ref, have, shift, cand, ext):
    at = device_at(place_ref)
    for slot in range(2):
        own = order_ref[2 * at + slot]
        for part in range(3):
            place = jnp.int32(len(have))
            for i, block in enumerate(have):
                place = jnp.where(block == own + (part + shift), i, place)
            ext[slot, part * BLK : (part + 1) * BLK, :] = cand[place]


def filter_kernel(
    n_in, place_ref, order_ref, q_own, kv_own, q_other, kv_other, w_own, w_other, *refs
):
    ins = refs[:n_in]
    pair_ref, high_ref, filt_ref, cand, grad, ext, lag = refs[n_in:]
    cg = jnp.zeros((ROWS, LANES), F32)
    for q_ref, kv_ref, w_ref in ((q_own, kv_own, w_own), (q_other, kv_other, w_other)):
        cg = cg + nt(q_ref[...], w_ref[0])
        cg = cg + nt(kv_ref[:, :HD], w_ref[1])
        cg = cg + nt(kv_ref[:, HD:], w_ref[2])
    grad[...] = cg.astype(BF).astype(F32)
    device = device_at(place_ref)
    partner = device + 1 - 2 * place_ref[3]
    first, second = order_ref[2 * device], order_ref[2 * device + 1]
    swapped = (first > second).astype(jnp.int32)
    low = grad[pl.ds(pl.multiple_of(swapped * BLK, BLK), BLK), :].astype(BF)
    high = grad[pl.ds(pl.multiple_of((1 - swapped) * BLK, BLK), BLK), :].astype(BF)
    high_ref[...] = high
    pair_ref[:BLK, :] = low
    pair_ref[BLK:, :] = high
    stack_blocks(ins, cand)
    have = [first, second] + blocks_at(order_ref, partner)
    have += blocks_at(order_ref, device - 2) + blocks_at(order_ref, partner - 2)
    have += low_high(order_ref, device + 2)[1:] + low_high(order_ref, partner + 2)[1:]
    extend(place_ref, order_ref, have, -2, cand, ext)
    for r in range(8):
        for slot in range(2):
            rows = [grad[slot * BLK + 8 * m : slot * BLK + 8 * m + 8, :] for m in range(BLK // 8)]
            last = 2 * BLK - r
            shifted = [ext[slot, last - TAPS + 8 + 8 * n : last - TAPS + 16 + 8 * n, :] for n in range(23)]
            for a in range(TAPS // 8):
                total = rows[0] * shifted[15 - a]
                for m in range(1, BLK // 8):
                    total = total + rows[m] * shifted[15 - a + m]
                j = 8 * a + r
                here = slice(8 * j, 8 * j + 8)
                lag[here, :] = total if slot == 0 else lag[here, :] + total
    taps = lag[pl.ds(0, TAPS, stride=8), :]
    for s in range(1, 8):
        taps = taps + lag[pl.ds(s, TAPS, stride=8), :]
    filt_ref[0] = taps.T


def project_and_filter(place, order, q_own, kv_own, q_other, kv_other, weight, w_other, ins):
    channels = ins[0].shape[1]
    tiles = channels // LANES
    half = tiles // 2
    whole = lambda a: pl.BlockSpec(a.shape, lambda i, p, o: (0, 0))
    column = lambda a: pl.BlockSpec((a.shape[0], LANES), lambda i, p, o: (0, i))
    which = lambda i, p, o: (jnp.where(i // half == p[3], 0, 1), lax.rem(i, half), 0)
    block = lambda rows: pl.BlockSpec((rows, LANES), lambda i, p, o: (0, i))
    blocks = sum(a.shape[0] // BLK for a in ins) + 1
    return pl.pallas_call(
        functools.partial(filter_kernel, len(ins)),
        grid_spec=pltpu.PrefetchScalarGridSpec(
            num_scalar_prefetch=2,
            grid=(tiles,),
            in_specs=[whole(a) for a in (q_own, kv_own, q_other, kv_other)]
            + [
                pl.BlockSpec((3, LANES, HD), lambda i, p, o: (0, p[4] * tiles + i, 0)),
                pl.BlockSpec((3, LANES, HD), lambda i, p, o: (0, i, 0)),
            ]
            + [column(a) for a in ins],
            out_specs=[block(ROWS), block(BLK), pl.BlockSpec((1, LANES, TAPS), which)],
            scratch_shapes=[
                pltpu.VMEM((blocks, BLK, LANES), F32),
                pltpu.VMEM((ROWS, LANES), F32),
                pltpu.VMEM((2, 3 * BLK, LANES), F32),
                pltpu.VMEM((8 * TAPS, LANES), F32),
            ],
        ),
        out_shape=[
            jax.ShapeDtypeStruct((ROWS, channels), BF),
            jax.ShapeDtypeStruct((BLK, channels), BF),
            jax.ShapeDtypeStruct((2, channels // 2, TAPS), F32),
        ],
        compiler_params=pltpu.CompilerParams(vmem_limit_bytes=40 << 20),
        cost_estimate=pl.CostEstimate(flops=4 << 30, bytes_accessed=8 << 20, transcendentals=0),
        name="project_and_filter",
    )(place, order, q_own, kv_own, q_other, kv_other, weight, w_other, *ins)


def conv_kernel(n_grad, place_ref, order_ref, *refs):
    grads = refs[:n_grad]
    filter_ref, out_ref, cand, ext, taps_ref = refs[n_grad:]
    taps_ref[...] = filter_ref[...].T
    stack_blocks(grads, cand)
    device = device_at(place_ref)
    partner = device + 1 - 2 * place_ref[3]
    have = low_high(order_ref, device) + low_high(order_ref, partner)
    have += low_high(order_ref, device + 2) + low_high(order_ref, partner + 2)
    have += low_high(order_ref, device - 2)[1:] + low_high(order_ref, partner - 2)[1:]
    extend(place_ref, order_ref, have, 0, cand, ext)
    for slot in range(2):
        acc = [jnp.zeros((8, LANES), F32) for _ in range(BLK // 8)]
        for r in range(8):
            shifted = [ext[slot, r + 8 * n : r + 8 * n + 8, :] for n in range(23)]
            for a in range(TAPS // 8):
                tap = taps_ref[8 * a + r : 8 * a + r + 1, :]
                for m in range(BLK // 8):
                    acc[m] = acc[m] + tap * shifted[m + a]
        out_ref[slot * BLK : (slot + 1) * BLK, :] = jnp.concatenate(acc, axis=0).astype(BF)


def input_conv(place, order, grads, taps):
    channels = taps.shape[0]
    column = lambda a: pl.BlockSpec((a.shape[0], LANES), lambda i, p, o: (0, i))
    blocks = sum(a.shape[0] // BLK for a in grads) + 1
    return pl.pallas_call(
        functools.partial(conv_kernel, len(grads)),
        grid_spec=pltpu.PrefetchScalarGridSpec(
            num_scalar_prefetch=2,
            grid=(channels // LANES,),
            in_specs=[column(a) for a in grads] + [pl.BlockSpec((LANES, TAPS), lambda i, p, o: (i, 0))],
            out_specs=pl.BlockSpec((ROWS, LANES), lambda i, p, o: (0, i)),
            scratch_shapes=[
                pltpu.VMEM((blocks, BLK, LANES), F32),
                pltpu.VMEM((2, 3 * BLK, LANES), F32),
                pltpu.VMEM((TAPS, LANES), F32),
            ],
        ),
        out_shape=jax.ShapeDtypeStruct((ROWS, channels), BF),
        compiler_params=pltpu.CompilerParams(vmem_limit_bytes=40 << 20),
        cost_estimate=pl.CostEstimate(flops=1 << 20, bytes_accessed=1 << 20, transcendentals=0),
        name="input_conv",
    )(place, order, *grads, taps)


def to_all(x, axes, count):
    return lax.all_to_all(jnp.broadcast_to(x[None], (count,) + x.shape), axes, 0, 0, tiled=True)


def swap(x, axis):
    return lax.ppermute(x, axis, [(0, 1), (1, 0)])


def from_ctx(x, distance):
    n = XL * Y * Z * CORE
    return lax.ppermute(x, CTX, [(i + distance, i) for i in range(n) if 0 <= i + distance < n])


def around(x, step, size, axis):
    return lax.ppermute(x, axis, [((i + step) % size, i) for i in range(size)])


def local(block_order, conv_input, conv_filter, query_rows, key_rows, value_rows, out_grad, qkv_weight):
    coords = [lax.axis_index(axis) for axis in CTX + ("head",)]
    core, head = coords[3], coords[4]
    channels = conv_input.shape[1]
    chips = XL * Y * Z
    entry = lax.iota(jnp.int32, 8)
    place = jnp.zeros((8,), jnp.int32)
    for i, coord in enumerate(coords):
        place = jnp.where(entry == i, coord, place)

    qg, kv = pack(query_rows, out_grad, key_rows, value_rows)
    qg = lax.all_to_all(qg, "z", 0, 0, tiled=True).reshape(NQ, 2 * HD)
    kv_xl = swap(kv, "xl")
    kv = jnp.concatenate((kv, kv_xl), axis=0)
    kv = jnp.concatenate([kv] + [around(kv, s, Y, "y") for s in range(1, Y)], axis=0)
    kv = jnp.concatenate((kv, swap(kv, "core")), axis=0)

    device = ((coords[0] * Y + coords[1]) * Z + coords[2]) * CORE + core
    ids = lax.dynamic_slice_in_dim(block_order, device * 2, 2, 0)
    swapped = (ids[0] > ids[1]).astype(jnp.int32)
    x_high = lax.dynamic_slice_in_dim(conv_input, (1 - swapped) * BLK, BLK, 0)
    w_sent = lax.dynamic_slice_in_dim(qkv_weight, (1 - head) * channels, channels, 1)
    w_sent, x_high, kv_xl = lax.optimization_barrier((w_sent, x_high, kv_xl))
    w_other = swap(w_sent, "head")

    stats = attention_stats(place, block_order, qg, kv)
    stats = lax.all_to_all(stats, "z", 0, 0, tiled=True)
    stats, w_other = lax.optimization_barrier((stats, w_other))
    dq, dkv_own, dkv_other = attention_grads(place, block_order, qg, kv, stats)

    dq, x_pair, x_high = lax.optimization_barrier((dq, conv_input, x_high))
    x_far = [from_ctx(x_pair, -2), from_ctx(x_high, 2)]
    dq_parts = lax.all_to_all(dq.reshape(Z, ROWS, HD), "z", 0, 0, tiled=True)
    dkv = (dkv_own + swap(dkv_other, "core")).astype(BF).reshape(XL * Y, ROWS, 2 * HD)
    dq_parts, dkv, x_far, x_pair = lax.optimization_barrier((dq_parts, dkv, x_far, x_pair))
    dkv_parts = lax.all_to_all(dkv, ("xl", "y"), 0, 0, tiled=True)
    x_swapped = [swap(x, "core") for x in [x_pair] + x_far]
    dkv_parts, x_swapped = lax.optimization_barrier((dkv_parts, x_swapped))
    query_grad = jnp.sum(dq_parts.astype(F32), axis=0).astype(BF)
    q_other = swap(query_grad, "head")
    kv_grad = jnp.sum(dkv_parts.astype(F32), axis=0).astype(BF)
    kv_other = swap(kv_grad, "head")

    ins = [conv_input, x_swapped[0], x_far[0], x_swapped[1], x_far[1], x_swapped[2]]
    g_pair, g_high, filter_part = project_and_filter(
        place, block_order, query_grad, kv_grad, q_other, kv_other, qkv_weight, w_other, ins
    )

    mine_sum = filter_part[0] + swap(filter_part[1], "core")
    far = [from_ctx(g_pair, 2), from_ctx(g_high, -2)]
    g_partner = swap(g_pair, "core")
    parts = lax.all_to_all(
        mine_sum.reshape(chips, channels // 2 // chips, TAPS), ("xl", "y", "z"), 0, 0, tiled=True
    )
    parts, far, g_partner = lax.optimization_barrier((parts, far, g_partner))
    total = jnp.sum(parts, axis=0)
    total, far = lax.optimization_barrier((total, far))
    grads = [g_pair, g_partner, far[0], swap(far[0], "core"), far[1], swap(far[1], "core")]
    half = to_all(total, ("xl", "y", "z"), chips)
    input_grad = input_conv(place, block_order, grads, conv_filter)
    half, input_grad = lax.optimization_barrier((half, input_grad))
    half = half.reshape(channels // 2, TAPS)
    other = swap(half, "core")
    filter_grad = jnp.concatenate(
        (jnp.where(core == 0, half, other), jnp.where(core == 0, other, half)), axis=0
    )
    return input_grad, filter_grad


def solution(mesh):
    fine = Mesh(mesh.devices.reshape(XL, Y, Z, CORE, HEAD), CTX + ("head",))
    rows = P(CTX, "head")
    return jax.shard_map(
        local,
        mesh=fine,
        in_specs=(P(), rows, P("head", None), rows, rows, rows, rows, P(None, None, "head")),
        out_specs=(rows, P("head", None)),
        check_vma=False,
    )
```

```python
import functools

import jax
import jax.numpy as jnp
from jax import lax
from jax.experimental import pallas as pl
from jax.experimental.pallas import tpu as pltpu
from jax.sharding import Mesh
from jax.sharding import PartitionSpec as P

HD = 128
TAPS = 128
BLK = 64
XL, Y, Z, CORE, HEAD = 2, 4, 8, 2, 2
ROWS = 2 * BLK
NQ = Z * ROWS
NK = XL * Y * CORE * ROWS
CTX = ("xl", "y", "z", "core")
LOWEST = -1e30
LOG2E = 1.4426950408889634
SCALE = HD**-0.5
QB = 1024
BF = jnp.bfloat16
F32 = jnp.float32
LANES = 128


def nt(a, b):
    return lax.dot_general(a, b, (((1,), (1,)), ((), ())), preferred_element_type=F32)


def tn(a, b):
    return lax.dot_general(a, b, (((0,), (0,)), ((), ())), preferred_element_type=F32)


def nn(a, b):
    return lax.dot_general(a, b, (((1,), (0,)), ((), ())), preferred_element_type=F32)


def block_of(order_ref, xl, y, z, core, slot):
    return order_ref[(((xl * Y + y) * Z + z) * CORE + core) * 2 + slot]


def fill_key_positions(place_ref, order_ref, kpos):
    row = lax.broadcasted_iota(jnp.int32, (BLK, LANES), 0)
    at = 0
    for c in range(CORE):
        for b in range(Y):
            for a in range(XL):
                xl = lax.rem(place_ref[0] + a, XL)
                y = lax.rem(place_ref[1] + b, Y)
                core = lax.rem(place_ref[3] + c, CORE)
                for slot in range(2):
                    block = block_of(order_ref, xl, y, place_ref[2], core, slot)
                    kpos[at : at + BLK, :] = row + block * BLK
                    at += BLK


def query_positions(place_ref, order_ref, step):
    lane = lax.broadcasted_iota(jnp.int32, (1, QB), 1)
    pos = jnp.zeros((1, QB), jnp.int32)
    for b in range(QB // BLK):
        at = step * (QB // BLK) + b
        block = block_of(order_ref, place_ref[0], place_ref[1], at // 2, place_ref[3], at % 2)
        pos = jnp.where(lane // BLK == b, block * BLK + lane % BLK, pos)
    return pos


def scores_t(q, k, kpos, qpos):
    s = nt(k, q) * (SCALE * LOG2E)
    seen = jnp.concatenate([kpos[...]] * (QB // LANES), axis=1) <= qpos
    return jnp.where(seen, s, LOWEST)


def stats_kernel(place_ref, order_ref, q_ref, g_ref, k_ref, v_ref, stat_ref, kpos):
    step = pl.program_id(0)

    @pl.when(step == 0)
    def _():
        fill_key_positions(place_ref, order_ref, kpos)

    s = scores_t(q_ref[...], k_ref[...], kpos, query_positions(place_ref, order_ref, step))
    dp = nt(v_ref[...], g_ref[...])
    top = jnp.max(s, axis=0, keepdims=True)
    w = jnp.exp2(s - top)
    norm = jnp.sum(w, axis=0, keepdims=True)
    cross = jnp.sum(w * dp, axis=0, keepdims=True)
    stat = jnp.concatenate((top + jnp.log2(norm), cross / norm), axis=0)
    stat_ref[...] = jnp.broadcast_to(stat[None], stat_ref.shape)


def grads_kernel(
    place_ref, order_ref, q_ref, g_ref, k_ref, v_ref, stat_ref, dq_ref, own_ref, other_ref, dk_acc, dv_acc, kpos
):
    step = pl.program_id(0)

    @pl.when(step == 0)
    def _():
        fill_key_positions(place_ref, order_ref, kpos)
        dk_acc[...] = jnp.zeros_like(dk_acc)
        dv_acc[...] = jnp.zeros_like(dv_acc)

    parts = stat_ref[:, 0, :]
    top = jnp.max(parts, axis=0, keepdims=True)
    lse = top + jnp.log2(jnp.sum(jnp.exp2(parts - top), axis=0, keepdims=True))
    delta = jnp.sum(jnp.exp2(parts - lse) * stat_ref[:, 1, :], axis=0, keepdims=True)
    q = q_ref[...]
    g = g_ref[...]
    s = scores_t(q, k_ref[...], kpos, query_positions(place_ref, order_ref, step))
    p = jnp.exp2(s - lse)
    dp = nt(v_ref[...], g)
    ds = (p * (dp - delta)).astype(BF)
    dv_acc[...] += nn(p.astype(BF), g)
    dk_acc[...] += nn(ds, q)
    dq_ref[...] = (SCALE * tn(ds, k_ref[...])).astype(dq_ref.dtype)

    @pl.when(step == pl.num_programs(0) - 1)
    def _():
        for at, ref in ((0, own_ref), (NK // 2, other_ref)):
            for b in range(Y):
                for a in range(XL):
                    owner = lax.rem(place_ref[0] + a, XL) * Y + lax.rem(place_ref[1] + b, Y)
                    here = pl.ds(at + (b * XL + a) * ROWS, ROWS)
                    there = pl.ds(pl.multiple_of(owner * ROWS, ROWS), ROWS)
                    ref[there, :HD] = SCALE * dk_acc[here, :]
                    ref[there, HD:] = dv_acc[here, :]


def attention_specs():
    rows = lambda col: pl.BlockSpec((QB, HD), lambda i, *_: (i, col))
    keys = lambda col: pl.BlockSpec((NK, HD), lambda i, *_: (0, col))
    return [
        rows(0),
        rows(1),
        keys(0),
        keys(1),
    ]


STAT = pl.BlockSpec((Z, 2, QB), lambda i, *_: (0, 0, i))


def attention_stats(place, order, qg, kv):
    return pl.pallas_call(
        stats_kernel,
        grid_spec=pltpu.PrefetchScalarGridSpec(
            num_scalar_prefetch=2,
            grid=(NQ // QB,),
            in_specs=attention_specs(),
            out_specs=STAT,
            scratch_shapes=[pltpu.VMEM((NK, LANES), jnp.int32)],
        ),
        out_shape=jax.ShapeDtypeStruct((Z, 2, NQ), F32),
        compiler_params=pltpu.CompilerParams(vmem_limit_bytes=40 << 20),
        cost_estimate=pl.CostEstimate(flops=4 * NQ * NK * HD, bytes_accessed=4 << 20, transcendentals=NQ * NK),
        name="attention_stats",
    )(place, order, qg, qg, kv, kv)


def attention_grads(place, order, qg, kv, stats):
    half = pl.BlockSpec((NK // 2, 2 * HD), lambda i, *_: (0, 0))
    return pl.pallas_call(
        grads_kernel,
        grid_spec=pltpu.PrefetchScalarGridSpec(
            num_scalar_prefetch=2,
            grid=(NQ // QB,),
            in_specs=attention_specs() + [STAT],
            out_specs=[pl.BlockSpec((QB, HD), lambda i, *_: (i, 0)), half, half],
            scratch_shapes=[
                pltpu.VMEM((NK, HD), F32),
                pltpu.VMEM((NK, HD), F32),
                pltpu.VMEM((NK, LANES), jnp.int32),
            ],
        ),
        out_shape=[
            jax.ShapeDtypeStruct((NQ, HD), BF),
            jax.ShapeDtypeStruct((NK // 2, 2 * HD), F32),
            jax.ShapeDtypeStruct((NK // 2, 2 * HD), F32),
        ],
        compiler_params=pltpu.CompilerParams(vmem_limit_bytes=40 << 20),
        cost_estimate=pl.CostEstimate(flops=10 * NQ * NK * HD, bytes_accessed=4 << 20, transcendentals=NQ * NK),
        name="attention_grads",
    )(place, order, qg, qg, kv, kv, stats)


def pack_kernel(q_ref, g_ref, k_ref, v_ref, qg_ref, kv_ref):
    kv_ref[:, :HD] = k_ref[...]
    kv_ref[:, HD:] = v_ref[...]
    for i in range(Z):
        qg_ref[i, :, :HD] = q_ref[...]
        qg_ref[i, :, HD:] = g_ref[...]


def pack(q, g, k, v):
    return pl.pallas_call(
        pack_kernel,
        out_shape=[jax.ShapeDtypeStruct((Z, ROWS, 2 * HD), BF), jax.ShapeDtypeStruct((ROWS, 2 * HD), BF)],
        name="pack",
    )(q, g, k, v)


def stack_blocks(refs, stack):
    at = 0
    for ref in refs:
        for b in range(ref.shape[0] // BLK):
            stack[at] = ref[b * BLK : (b + 1) * BLK, :].astype(F32)
            at += 1
    stack[at] = jnp.zeros((BLK, LANES), F32)


def device_at(place_ref):
    return ((place_ref[0] * Y + place_ref[1]) * Z + place_ref[2]) * CORE + place_ref[3]


def blocks_at(order_ref, at):
    inside = jnp.logical_and(at >= 0, at < XL * Y * Z * CORE)
    at = jnp.where(inside, at, 0)
    return [jnp.where(inside, order_ref[2 * at + slot], -1000) for slot in range(2)]


def low_high(order_ref, at):
    first, second = blocks_at(order_ref, at)
    return [jnp.minimum(first, second), jnp.maximum(first, second)]


def extend(place_ref, order_ref, have, shift, cand, ext):
    at = device_at(place_ref)
    for slot in range(2):
        own = order_ref[2 * at + slot]
        for part in range(3):
            place = jnp.int32(len(have))
            for i, block in enumerate(have):
                place = jnp.where(block == own + (part + shift), i, place)
            ext[slot, part * BLK : (part + 1) * BLK, :] = cand[place]


def filter_kernel(
    n_in, place_ref, order_ref, q_own, kv_own, q_other, kv_other, w_own, w_other, *refs
):
    ins = refs[:n_in]
    pair_ref, high_ref, filt_ref, cand, projected, grad, ext, lag = refs[n_in:]
    step = pl.program_id(0)

    @pl.when(step == 0)
    def _():
        cg = jnp.zeros((ROWS, w_own.shape[1]), F32)
        for q_ref, kv_ref, w_ref in ((q_own, kv_own, w_own), (q_other, kv_other, w_other)):
            cg = cg + nt(q_ref[...], w_ref[0])
            cg = cg + nt(kv_ref[:, :HD], w_ref[1])
            cg = cg + nt(kv_ref[:, HD:], w_ref[2])
        cg = cg.astype(BF).astype(F32)
        for tile in range(w_own.shape[1] // LANES):
            projected[tile] = cg[:, tile * LANES : (tile + 1) * LANES]

    grad[...] = projected[step]
    device = device_at(place_ref)
    partner = device + 1 - 2 * place_ref[3]
    first, second = order_ref[2 * device], order_ref[2 * device + 1]
    swapped = (first > second).astype(jnp.int32)
    low = grad[pl.ds(pl.multiple_of(swapped * BLK, BLK), BLK), :].astype(BF)
    high = grad[pl.ds(pl.multiple_of((1 - swapped) * BLK, BLK), BLK), :].astype(BF)
    high_ref[...] = high
    pair_ref[:BLK, :] = low
    pair_ref[BLK:, :] = high
    stack_blocks(ins, cand)
    have = [first, second] + blocks_at(order_ref, partner)
    have += blocks_at(order_ref, device - 2) + blocks_at(order_ref, partner - 2)
    have += low_high(order_ref, device + 2)[1:] + low_high(order_ref, partner + 2)[1:]
    extend(place_ref, order_ref, have, -2, cand, ext)
    for r in range(8):
        totals = [None] * (TAPS // 8)
        for slot in range(2):
            rows = [grad[slot * BLK + 8 * m : slot * BLK + 8 * m + 8, :] for m in range(BLK // 8)]
            last = 2 * BLK - r
            shifted = [ext[slot, last - TAPS + 8 + 8 * n : last - TAPS + 16 + 8 * n, :] for n in range(23)]
            for a in range(TAPS // 8):
                for m in range(BLK // 8):
                    term = rows[m] * shifted[15 - a + m]
                    totals[a] = term if totals[a] is None else totals[a] + term
        for a in range(TAPS // 8):
            j = 8 * a + r
            lag[8 * j : 8 * j + 8, :] = totals[a]
    taps = lag[pl.ds(0, TAPS, stride=8), :]
    for s in range(1, 8):
        taps = taps + lag[pl.ds(s, TAPS, stride=8), :]
    filt_ref[0] = taps.T


def project_and_filter(place, order, q_own, kv_own, q_other, kv_other, weight, w_other, ins):
    channels = ins[0].shape[1]
    tiles = channels // LANES
    half = tiles // 2
    whole = lambda a: pl.BlockSpec(a.shape, lambda i, p, o: (0, 0))
    column = lambda a: pl.BlockSpec((a.shape[0], LANES), lambda i, p, o: (0, i))
    which = lambda i, p, o: (jnp.where(i // half == p[3], 0, 1), lax.rem(i, half), 0)
    block = lambda rows: pl.BlockSpec((rows, LANES), lambda i, p, o: (0, i))
    blocks = sum(a.shape[0] // BLK for a in ins) + 1
    return pl.pallas_call(
        functools.partial(filter_kernel, len(ins)),
        grid_spec=pltpu.PrefetchScalarGridSpec(
            num_scalar_prefetch=2,
            grid=(tiles,),
            in_specs=[whole(a) for a in (q_own, kv_own, q_other, kv_other)]
            + [
                pl.BlockSpec((3, channels, HD), lambda i, p, o: (0, p[4], 0)),
                pl.BlockSpec((3, channels, HD), lambda i, p, o: (0, 0, 0)),
            ]
            + [column(a) for a in ins],
            out_specs=[block(ROWS), block(BLK), pl.BlockSpec((1, LANES, TAPS), which)],
            scratch_shapes=[
                pltpu.VMEM((blocks, BLK, LANES), F32),
                pltpu.VMEM((tiles, ROWS, LANES), F32),
                pltpu.VMEM((ROWS, LANES), F32),
                pltpu.VMEM((2, 3 * BLK, LANES), F32),
                pltpu.VMEM((8 * TAPS, LANES), F32),
            ],
        ),
        out_shape=[
            jax.ShapeDtypeStruct((ROWS, channels), BF),
            jax.ShapeDtypeStruct((BLK, channels), BF),
            jax.ShapeDtypeStruct((2, channels // 2, TAPS), F32),
        ],
        compiler_params=pltpu.CompilerParams(vmem_limit_bytes=40 << 20),
        cost_estimate=pl.CostEstimate(flops=4 << 30, bytes_accessed=8 << 20, transcendentals=0),
        name="project_and_filter",
    )(place, order, q_own, kv_own, q_other, kv_other, weight, w_other, *ins)


def conv_kernel(n_grad, place_ref, order_ref, *refs):
    grads = refs[:n_grad]
    filter_ref, out_ref, cand, ext, taps_ref = refs[n_grad:]
    taps_ref[...] = filter_ref[...].T
    stack_blocks(grads, cand)
    device = device_at(place_ref)
    partner = device + 1 - 2 * place_ref[3]
    have = low_high(order_ref, device) + low_high(order_ref, partner)
    have += low_high(order_ref, device + 2) + low_high(order_ref, partner + 2)
    have += low_high(order_ref, device - 2)[1:] + low_high(order_ref, partner - 2)[1:]
    extend(place_ref, order_ref, have, 0, cand, ext)
    for slot in range(2):
        acc = [jnp.zeros((8, LANES), F32) for _ in range(BLK // 8)]
        for r in range(8):
            shifted = [ext[slot, r + 8 * n : r + 8 * n + 8, :] for n in range(23)]
            for a in range(TAPS // 8):
                tap = taps_ref[8 * a + r : 8 * a + r + 1, :]
                for m in range(BLK // 8):
                    acc[m] = acc[m] + tap * shifted[m + a]
        out_ref[slot * BLK : (slot + 1) * BLK, :] = jnp.concatenate(acc, axis=0).astype(BF)


def input_conv(place, order, grads, taps):
    channels = taps.shape[0]
    column = lambda a: pl.BlockSpec((a.shape[0], LANES), lambda i, p, o: (0, i))
    blocks = sum(a.shape[0] // BLK for a in grads) + 1
    return pl.pallas_call(
        functools.partial(conv_kernel, len(grads)),
        grid_spec=pltpu.PrefetchScalarGridSpec(
            num_scalar_prefetch=2,
            grid=(channels // LANES,),
            in_specs=[column(a) for a in grads] + [pl.BlockSpec((LANES, TAPS), lambda i, p, o: (i, 0))],
            out_specs=pl.BlockSpec((ROWS, LANES), lambda i, p, o: (0, i)),
            scratch_shapes=[
                pltpu.VMEM((blocks, BLK, LANES), F32),
                pltpu.VMEM((2, 3 * BLK, LANES), F32),
                pltpu.VMEM((TAPS, LANES), F32),
            ],
        ),
        out_shape=jax.ShapeDtypeStruct((ROWS, channels), BF),
        compiler_params=pltpu.CompilerParams(vmem_limit_bytes=40 << 20),
        cost_estimate=pl.CostEstimate(flops=1 << 20, bytes_accessed=1 << 20, transcendentals=0),
        name="input_conv",
    )(place, order, *grads, taps)


def to_all(x, axes, count):
    return lax.all_to_all(jnp.broadcast_to(x[None], (count,) + x.shape), axes, 0, 0, tiled=True)


def swap(x, axis):
    return lax.ppermute(x, axis, [(0, 1), (1, 0)])


def from_ctx(x, distance):
    n = XL * Y * Z * CORE
    return lax.ppermute(x, CTX, [(i + distance, i) for i in range(n) if 0 <= i + distance < n])


def around(x, step, size, axis):
    return lax.ppermute(x, axis, [((i + step) % size, i) for i in range(size)])


def local(block_order, conv_input, conv_filter, query_rows, key_rows, value_rows, out_grad, qkv_weight):
    coords = [lax.axis_index(axis) for axis in CTX + ("head",)]
    core, head = coords[3], coords[4]
    channels = conv_input.shape[1]
    chips = XL * Y * Z
    entry = lax.iota(jnp.int32, 8)
    place = jnp.zeros((8,), jnp.int32)
    for i, coord in enumerate(coords):
        place = jnp.where(entry == i, coord, place)

    qg, kv = pack(query_rows, out_grad, key_rows, value_rows)
    qg = lax.all_to_all(qg, "z", 0, 0, tiled=True).reshape(NQ, 2 * HD)
    kv_xl = swap(kv, "xl")
    kv = jnp.concatenate((kv, kv_xl), axis=0)
    kv = jnp.concatenate([kv] + [around(kv, s, Y, "y") for s in range(1, Y)], axis=0)
    kv = jnp.concatenate((kv, swap(kv, "core")), axis=0)

    device = ((coords[0] * Y + coords[1]) * Z + coords[2]) * CORE + core
    ids = lax.dynamic_slice_in_dim(block_order, device * 2, 2, 0)
    swapped = (ids[0] > ids[1]).astype(jnp.int32)
    x_high = lax.dynamic_slice_in_dim(conv_input, (1 - swapped) * BLK, BLK, 0)
    w_sent = lax.dynamic_slice_in_dim(qkv_weight, (1 - head) * channels, channels, 1)
    w_sent, x_high, kv_xl = lax.optimization_barrier((w_sent, x_high, kv_xl))
    w_other = swap(w_sent, "head")

    stats = attention_stats(place, block_order, qg, kv)
    stats = lax.all_to_all(stats, "z", 0, 0, tiled=True)
    stats, w_other = lax.optimization_barrier((stats, w_other))
    dq, dkv_own, dkv_other = attention_grads(place, block_order, qg, kv, stats)

    dq, x_pair, x_high = lax.optimization_barrier((dq, conv_input, x_high))
    x_far = [from_ctx(x_pair, -2), from_ctx(x_high, 2)]
    dq_parts = lax.all_to_all(dq.reshape(Z, ROWS, HD), "z", 0, 0, tiled=True)
    dkv = (dkv_own + swap(dkv_other, "core")).astype(BF).reshape(XL * Y, ROWS, 2 * HD)
    dq_parts, dkv, x_far, x_pair = lax.optimization_barrier((dq_parts, dkv, x_far, x_pair))
    dkv_parts = lax.all_to_all(dkv, ("xl", "y"), 0, 0, tiled=True)
    x_swapped = [swap(x, "core") for x in [x_pair] + x_far]
    dkv_parts, x_swapped = lax.optimization_barrier((dkv_parts, x_swapped))
    query_grad = jnp.sum(dq_parts.astype(F32), axis=0).astype(BF)
    q_other = swap(query_grad, "head")
    kv_grad = jnp.sum(dkv_parts.astype(F32), axis=0).astype(BF)
    kv_other = swap(kv_grad, "head")

    ins = [conv_input, x_swapped[0], x_far[0], x_swapped[1], x_far[1], x_swapped[2]]
    g_pair, g_high, filter_part = project_and_filter(
        place, block_order, query_grad, kv_grad, q_other, kv_other, qkv_weight, w_other, ins
    )

    mine_sum = filter_part[0] + swap(filter_part[1], "core")
    far = [from_ctx(g_pair, 2), from_ctx(g_high, -2)]
    g_partner = swap(g_pair, "core")
    parts = lax.all_to_all(
        mine_sum.reshape(chips, channels // 2 // chips, TAPS), ("xl", "y", "z"), 0, 0, tiled=True
    )
    parts, far, g_partner = lax.optimization_barrier((parts, far, g_partner))
    total = jnp.sum(parts, axis=0)
    total, far = lax.optimization_barrier((total, far))
    grads = [g_pair, g_partner, far[0], swap(far[0], "core"), far[1], swap(far[1], "core")]
    half = to_all(total, ("xl", "y", "z"), chips)
    input_grad = input_conv(place, block_order, grads, conv_filter)
    half, input_grad = lax.optimization_barrier((half, input_grad))
    half = half.reshape(channels // 2, TAPS)
    other = swap(half, "core")
    filter_grad = jnp.concatenate(
        (jnp.where(core == 0, half, other), jnp.where(core == 0, other, half)), axis=0
    )
    return input_grad, filter_grad


def solution(mesh):
    fine = Mesh(mesh.devices.reshape(XL, Y, Z, CORE, HEAD), CTX + ("head",))
    rows = P(CTX, "head")
    return jax.shard_map(
        local,
        mesh=fine,
        in_specs=(P(), rows, P("head", None), rows, rows, rows, rows, P(None, None, "head")),
        out_specs=(rows, P("head", None)),
        check_vma=False,
    )
```

```python
import functools

import jax
import jax.numpy as jnp
from jax import lax
from jax.experimental import pallas as pl
from jax.experimental.pallas import tpu as pltpu
from jax.sharding import Mesh
from jax.sharding import PartitionSpec as P

HD = 128
TAPS = 128
BLK = 64
XL, Y, Z, CORE, HEAD = 2, 4, 8, 2, 2
ROWS = 2 * BLK
NQ = Z * ROWS
NK = XL * Y * CORE * ROWS
CTX = ("xl", "y", "z", "core")
LOWEST = -1e30
LOG2E = 1.4426950408889634
SCALE = HD**-0.5
QB = 1024
BF = jnp.bfloat16
F32 = jnp.float32
LANES = 128


def nt(a, b):
    return lax.dot_general(a, b, (((1,), (1,)), ((), ())), preferred_element_type=F32)


def tn(a, b):
    return lax.dot_general(a, b, (((0,), (0,)), ((), ())), preferred_element_type=F32)


def nn(a, b):
    return lax.dot_general(a, b, (((1,), (0,)), ((), ())), preferred_element_type=F32)


def block_of(order_ref, xl, y, z, core, slot):
    return order_ref[(((xl * Y + y) * Z + z) * CORE + core) * 2 + slot]


def fill_key_positions(place_ref, order_ref, kpos):
    row = lax.broadcasted_iota(jnp.int32, (BLK, LANES), 0)
    at = 0
    for c in range(CORE):
        for b in range(Y):
            for a in range(XL):
                xl = lax.rem(place_ref[0] + a, XL)
                y = lax.rem(place_ref[1] + b, Y)
                core = lax.rem(place_ref[3] + c, CORE)
                for slot in range(2):
                    block = block_of(order_ref, xl, y, place_ref[2], core, slot)
                    kpos[at : at + BLK, :] = row + block * BLK
                    at += BLK


def query_positions(place_ref, order_ref, step):
    lane = lax.broadcasted_iota(jnp.int32, (1, QB), 1)
    pos = jnp.zeros((1, QB), jnp.int32)
    for b in range(QB // BLK):
        at = step * (QB // BLK) + b
        block = block_of(order_ref, place_ref[0], place_ref[1], at // 2, place_ref[3], at % 2)
        pos = jnp.where(lane // BLK == b, block * BLK + lane % BLK, pos)
    return pos


def scores_t(q, k, kpos, qpos):
    s = nt(k, q) * (SCALE * LOG2E)
    seen = jnp.concatenate([kpos[...]] * (QB // LANES), axis=1) <= qpos
    return jnp.where(seen, s, LOWEST)


def stats_kernel(place_ref, order_ref, q_ref, g_ref, k_ref, v_ref, stat_ref, kpos):
    step = pl.program_id(0)

    @pl.when(step == 0)
    def _():
        fill_key_positions(place_ref, order_ref, kpos)

    s = scores_t(q_ref[...], k_ref[...], kpos, query_positions(place_ref, order_ref, step))
    dp = nt(v_ref[...], g_ref[...])
    top = jnp.max(s, axis=0, keepdims=True)
    w = jnp.exp2(s - top)
    norm = jnp.sum(w, axis=0, keepdims=True)
    cross = jnp.sum(w * dp, axis=0, keepdims=True)
    stat = jnp.concatenate((top + jnp.log2(norm), cross / norm), axis=0)
    stat_ref[...] = jnp.broadcast_to(stat[None], stat_ref.shape)


def grads_kernel(
    place_ref, order_ref, q_ref, g_ref, k_ref, v_ref, stat_ref, dq_ref, own_ref, other_ref, dk_acc, dv_acc, kpos
):
    step = pl.program_id(0)

    @pl.when(step == 0)
    def _():
        fill_key_positions(place_ref, order_ref, kpos)
        dk_acc[...] = jnp.zeros_like(dk_acc)
        dv_acc[...] = jnp.zeros_like(dv_acc)

    parts = stat_ref[:, 0, :]
    top = jnp.max(parts, axis=0, keepdims=True)
    lse = top + jnp.log2(jnp.sum(jnp.exp2(parts - top), axis=0, keepdims=True))
    delta = jnp.sum(jnp.exp2(parts - lse) * stat_ref[:, 1, :], axis=0, keepdims=True)
    q = q_ref[...]
    g = g_ref[...]
    s = scores_t(q, k_ref[...], kpos, query_positions(place_ref, order_ref, step))
    p = jnp.exp2(s - lse)
    dp = nt(v_ref[...], g)
    ds = (p * (dp - delta)).astype(BF)
    dv_acc[...] += nn(p.astype(BF), g)
    dk_acc[...] += nn(ds, q)
    dq_ref[...] = (SCALE * tn(ds, k_ref[...])).astype(dq_ref.dtype)

    @pl.when(step == pl.num_programs(0) - 1)
    def _():
        for at, ref in ((0, own_ref), (NK // 2, other_ref)):
            for b in range(Y):
                for a in range(XL):
                    owner = lax.rem(place_ref[0] + a, XL) * Y + lax.rem(place_ref[1] + b, Y)
                    here = pl.ds(at + (b * XL + a) * ROWS, ROWS)
                    there = pl.ds(pl.multiple_of(owner * ROWS, ROWS), ROWS)
                    ref[there, :HD] = SCALE * dk_acc[here, :]
                    ref[there, HD:] = dv_acc[here, :]


def attention_specs():
    rows = lambda col: pl.BlockSpec((QB, HD), lambda i, *_: (i, col))
    keys = lambda col: pl.BlockSpec((NK, HD), lambda i, *_: (0, col))
    return [
        rows(0),
        rows(1),
        keys(0),
        keys(1),
    ]


STAT = pl.BlockSpec((Z, 2, QB), lambda i, *_: (0, 0, i))


def attention_stats(place, order, qg, kv):
    return pl.pallas_call(
        stats_kernel,
        grid_spec=pltpu.PrefetchScalarGridSpec(
            num_scalar_prefetch=2,
            grid=(NQ // QB,),
            in_specs=attention_specs(),
            out_specs=STAT,
            scratch_shapes=[pltpu.VMEM((NK, LANES), jnp.int32)],
        ),
        out_shape=jax.ShapeDtypeStruct((Z, 2, NQ), F32),
        compiler_params=pltpu.CompilerParams(vmem_limit_bytes=56 << 20),
        cost_estimate=pl.CostEstimate(flops=4 * NQ * NK * HD, bytes_accessed=4 << 20, transcendentals=NQ * NK),
        name="attention_stats",
    )(place, order, qg, qg, kv, kv)


def attention_grads(place, order, qg, kv, stats):
    half = pl.BlockSpec((NK // 2, 2 * HD), lambda i, *_: (0, 0))
    return pl.pallas_call(
        grads_kernel,
        grid_spec=pltpu.PrefetchScalarGridSpec(
            num_scalar_prefetch=2,
            grid=(NQ // QB,),
            in_specs=attention_specs() + [STAT],
            out_specs=[pl.BlockSpec((QB, HD), lambda i, *_: (i, 0)), half, half],
            scratch_shapes=[
                pltpu.VMEM((NK, HD), F32),
                pltpu.VMEM((NK, HD), F32),
                pltpu.VMEM((NK, LANES), jnp.int32),
            ],
        ),
        out_shape=[
            jax.ShapeDtypeStruct((NQ, HD), BF),
            jax.ShapeDtypeStruct((NK // 2, 2 * HD), F32),
            jax.ShapeDtypeStruct((NK // 2, 2 * HD), F32),
        ],
        compiler_params=pltpu.CompilerParams(vmem_limit_bytes=56 << 20),
        cost_estimate=pl.CostEstimate(flops=10 * NQ * NK * HD, bytes_accessed=4 << 20, transcendentals=NQ * NK),
        name="attention_grads",
    )(place, order, qg, qg, kv, kv, stats)


def pack_kernel(q_ref, g_ref, k_ref, v_ref, qg_ref, kv_ref):
    kv_ref[:, :HD] = k_ref[...]
    kv_ref[:, HD:] = v_ref[...]
    for i in range(Z):
        qg_ref[i, :, :HD] = q_ref[...]
        qg_ref[i, :, HD:] = g_ref[...]


def pack(q, g, k, v):
    return pl.pallas_call(
        pack_kernel,
        out_shape=[jax.ShapeDtypeStruct((Z, ROWS, 2 * HD), BF), jax.ShapeDtypeStruct((ROWS, 2 * HD), BF)],
        name="pack",
    )(q, g, k, v)


def stack_blocks(refs, stack):
    at = 0
    for ref in refs:
        for b in range(ref.shape[0] // BLK):
            stack[at] = ref[b * BLK : (b + 1) * BLK, :].astype(F32)
            at += 1
    stack[at] = jnp.zeros((BLK, LANES), F32)


def device_at(place_ref):
    return ((place_ref[0] * Y + place_ref[1]) * Z + place_ref[2]) * CORE + place_ref[3]


def blocks_at(order_ref, at):
    inside = jnp.logical_and(at >= 0, at < XL * Y * Z * CORE)
    at = jnp.where(inside, at, 0)
    return [jnp.where(inside, order_ref[2 * at + slot], -1000) for slot in range(2)]


def low_high(order_ref, at):
    first, second = blocks_at(order_ref, at)
    return [jnp.minimum(first, second), jnp.maximum(first, second)]


def extend(place_ref, order_ref, have, shift, cand, ext):
    at = device_at(place_ref)
    for slot in range(2):
        own = order_ref[2 * at + slot]
        for part in range(3):
            place = jnp.int32(len(have))
            for i, block in enumerate(have):
                place = jnp.where(block == own + (part + shift), i, place)
            ext[slot, part * BLK : (part + 1) * BLK, :] = cand[place]


def filter_kernel(
    n_in, place_ref, order_ref, q_own, kv_own, q_other, kv_other, w_own, w_other, *refs
):
    ins = refs[:n_in]
    pair_ref, high_ref, filt_ref, cand, projected, grad, ext, lag = refs[n_in:]
    step = pl.program_id(0)

    @pl.when(step == 0)
    def _():
        cg = jnp.zeros((ROWS, w_own.shape[1]), F32)
        for q_ref, kv_ref, w_ref in ((q_own, kv_own, w_own), (q_other, kv_other, w_other)):
            cg = cg + nt(q_ref[...], w_ref[0])
            cg = cg + nt(kv_ref[:, :HD], w_ref[1])
            cg = cg + nt(kv_ref[:, HD:], w_ref[2])
        cg = cg.astype(BF).astype(F32)
        for tile in range(w_own.shape[1] // LANES):
            projected[tile] = cg[:, tile * LANES : (tile + 1) * LANES]

    grad[...] = projected[step]
    device = device_at(place_ref)
    partner = device + 1 - 2 * place_ref[3]
    first, second = order_ref[2 * device], order_ref[2 * device + 1]
    swapped = (first > second).astype(jnp.int32)
    low = grad[pl.ds(pl.multiple_of(swapped * BLK, BLK), BLK), :].astype(BF)
    high = grad[pl.ds(pl.multiple_of((1 - swapped) * BLK, BLK), BLK), :].astype(BF)
    high_ref[...] = high
    pair_ref[:BLK, :] = low
    pair_ref[BLK:, :] = high
    stack_blocks(ins, cand)
    have = [first, second] + blocks_at(order_ref, partner)
    have += blocks_at(order_ref, device - 2) + blocks_at(order_ref, partner - 2)
    have += low_high(order_ref, device + 2)[1:] + low_high(order_ref, partner + 2)[1:]
    extend(place_ref, order_ref, have, -2, cand, ext)
    for r in range(8):
        totals = [None] * (TAPS // 8)
        for slot in range(2):
            rows = [grad[slot * BLK + 8 * m : slot * BLK + 8 * m + 8, :] for m in range(BLK // 8)]
            last = 2 * BLK - r
            shifted = [ext[slot, last - TAPS + 8 + 8 * n : last - TAPS + 16 + 8 * n, :] for n in range(23)]
            for a in range(TAPS // 8):
                for m in range(BLK // 8):
                    term = rows[m] * shifted[15 - a + m]
                    totals[a] = term if totals[a] is None else totals[a] + term
        for a in range(TAPS // 8):
            j = 8 * a + r
            lag[8 * j : 8 * j + 8, :] = totals[a]
    taps = lag[pl.ds(0, TAPS, stride=8), :]
    for s in range(1, 8):
        taps = taps + lag[pl.ds(s, TAPS, stride=8), :]
    filt_ref[0] = taps.T


def project_and_filter(place, order, q_own, kv_own, q_other, kv_other, weight, w_other, ins):
    channels = ins[0].shape[1]
    tiles = channels // LANES
    half = tiles // 2
    whole = lambda a: pl.BlockSpec(a.shape, lambda i, p, o: (0, 0))
    column = lambda a: pl.BlockSpec((a.shape[0], LANES), lambda i, p, o: (0, i))
    which = lambda i, p, o: (jnp.where(i // half == p[3], 0, 1), lax.rem(i, half), 0)
    block = lambda rows: pl.BlockSpec((rows, LANES), lambda i, p, o: (0, i))
    blocks = sum(a.shape[0] // BLK for a in ins) + 1
    return pl.pallas_call(
        functools.partial(filter_kernel, len(ins)),
        grid_spec=pltpu.PrefetchScalarGridSpec(
            num_scalar_prefetch=2,
            grid=(tiles,),
            in_specs=[whole(a) for a in (q_own, kv_own, q_other, kv_other)]
            + [
                pl.BlockSpec((3, channels, HD), lambda i, p, o: (0, p[4], 0)),
                pl.BlockSpec((3, channels, HD), lambda i, p, o: (0, 0, 0)),
            ]
            + [column(a) for a in ins],
            out_specs=[block(ROWS), block(BLK), pl.BlockSpec((1, LANES, TAPS), which)],
            scratch_shapes=[
                pltpu.VMEM((blocks, BLK, LANES), F32),
                pltpu.VMEM((tiles, ROWS, LANES), F32),
                pltpu.VMEM((ROWS, LANES), F32),
                pltpu.VMEM((2, 3 * BLK, LANES), F32),
                pltpu.VMEM((8 * TAPS, LANES), F32),
            ],
        ),
        out_shape=[
            jax.ShapeDtypeStruct((ROWS, channels), BF),
            jax.ShapeDtypeStruct((BLK, channels), BF),
            jax.ShapeDtypeStruct((2, channels // 2, TAPS), F32),
        ],
        compiler_params=pltpu.CompilerParams(vmem_limit_bytes=56 << 20),
        cost_estimate=pl.CostEstimate(flops=4 << 30, bytes_accessed=8 << 20, transcendentals=0),
        name="project_and_filter",
    )(place, order, q_own, kv_own, q_other, kv_other, weight, w_other, *ins)


def conv_kernel(n_grad, place_ref, order_ref, *refs):
    grads = refs[:n_grad]
    filter_ref, out_ref, cand, ext, taps_ref = refs[n_grad:]
    taps_ref[...] = filter_ref[...].T
    stack_blocks(grads, cand)
    device = device_at(place_ref)
    partner = device + 1 - 2 * place_ref[3]
    have = low_high(order_ref, device) + low_high(order_ref, partner)
    have += low_high(order_ref, device + 2) + low_high(order_ref, partner + 2)
    have += low_high(order_ref, device - 2)[1:] + low_high(order_ref, partner - 2)[1:]
    extend(place_ref, order_ref, have, 0, cand, ext)
    for slot in range(2):
        acc = [jnp.zeros((8, LANES), F32) for _ in range(BLK // 8)]
        for r in range(8):
            shifted = [ext[slot, r + 8 * n : r + 8 * n + 8, :] for n in range(23)]
            for a in range(TAPS // 8):
                tap = taps_ref[8 * a + r : 8 * a + r + 1, :]
                for m in range(BLK // 8):
                    acc[m] = acc[m] + tap * shifted[m + a]
        out_ref[slot * BLK : (slot + 1) * BLK, :] = jnp.concatenate(acc, axis=0).astype(BF)


def input_conv(place, order, grads, taps):
    channels = taps.shape[0]
    column = lambda a: pl.BlockSpec((a.shape[0], LANES), lambda i, p, o: (0, i))
    blocks = sum(a.shape[0] // BLK for a in grads) + 1
    return pl.pallas_call(
        functools.partial(conv_kernel, len(grads)),
        grid_spec=pltpu.PrefetchScalarGridSpec(
            num_scalar_prefetch=2,
            grid=(channels // LANES,),
            in_specs=[column(a) for a in grads] + [pl.BlockSpec((LANES, TAPS), lambda i, p, o: (i, 0))],
            out_specs=pl.BlockSpec((ROWS, LANES), lambda i, p, o: (0, i)),
            scratch_shapes=[
                pltpu.VMEM((blocks, BLK, LANES), F32),
                pltpu.VMEM((2, 3 * BLK, LANES), F32),
                pltpu.VMEM((TAPS, LANES), F32),
            ],
        ),
        out_shape=jax.ShapeDtypeStruct((ROWS, channels), BF),
        compiler_params=pltpu.CompilerParams(vmem_limit_bytes=56 << 20),
        cost_estimate=pl.CostEstimate(flops=1 << 20, bytes_accessed=1 << 20, transcendentals=0),
        name="input_conv",
    )(place, order, *grads, taps)


def to_all(x, axes, count):
    return lax.all_to_all(jnp.broadcast_to(x[None], (count,) + x.shape), axes, 0, 0, tiled=True)


def swap(x, axis):
    return lax.ppermute(x, axis, [(0, 1), (1, 0)])


def from_ctx(x, distance):
    n = XL * Y * Z * CORE
    return lax.ppermute(x, CTX, [(i + distance, i) for i in range(n) if 0 <= i + distance < n])


def around(x, step, size, axis):
    return lax.ppermute(x, axis, [((i + step) % size, i) for i in range(size)])


def local(block_order, conv_input, conv_filter, query_rows, key_rows, value_rows, out_grad, qkv_weight):
    coords = [lax.axis_index(axis) for axis in CTX + ("head",)]
    core, head = coords[3], coords[4]
    channels = conv_input.shape[1]
    chips = XL * Y * Z
    entry = lax.iota(jnp.int32, 8)
    place = jnp.zeros((8,), jnp.int32)
    for i, coord in enumerate(coords):
        place = jnp.where(entry == i, coord, place)

    qg, kv = pack(query_rows, out_grad, key_rows, value_rows)
    qg = lax.all_to_all(qg, "z", 0, 0, tiled=True).reshape(NQ, 2 * HD)
    kv_xl = swap(kv, "xl")
    kv = jnp.concatenate((kv, kv_xl), axis=0)
    kv = jnp.concatenate([kv] + [around(kv, s, Y, "y") for s in range(1, Y)], axis=0)
    kv = jnp.concatenate((kv, swap(kv, "core")), axis=0)

    device = ((coords[0] * Y + coords[1]) * Z + coords[2]) * CORE + core
    ids = lax.dynamic_slice_in_dim(block_order, device * 2, 2, 0)
    swapped = (ids[0] > ids[1]).astype(jnp.int32)
    x_high = lax.dynamic_slice_in_dim(conv_input, (1 - swapped) * BLK, BLK, 0)
    w_sent = lax.dynamic_slice_in_dim(qkv_weight, (1 - head) * channels, channels, 1)
    w_sent, x_high, kv_xl = lax.optimization_barrier((w_sent, x_high, kv_xl))
    w_other = swap(w_sent, "head")

    stats = attention_stats(place, block_order, qg, kv)
    stats = lax.all_to_all(stats, "z", 0, 0, tiled=True)
    stats, w_other = lax.optimization_barrier((stats, w_other))
    dq, dkv_own, dkv_other = attention_grads(place, block_order, qg, kv, stats)

    dq, x_pair, x_high = lax.optimization_barrier((dq, conv_input, x_high))
    x_far = [from_ctx(x_pair, -2), from_ctx(x_high, 2)]
    dq_parts = lax.all_to_all(dq.reshape(Z, ROWS, HD), "z", 0, 0, tiled=True)
    dkv = (dkv_own + swap(dkv_other, "core")).astype(BF).reshape(XL * Y, ROWS, 2 * HD)
    dq_parts, dkv, x_far, x_pair = lax.optimization_barrier((dq_parts, dkv, x_far, x_pair))
    dkv_parts = lax.all_to_all(dkv, ("xl", "y"), 0, 0, tiled=True)
    x_swapped = [swap(x, "core") for x in [x_pair] + x_far]
    dkv_parts, x_swapped = lax.optimization_barrier((dkv_parts, x_swapped))
    query_grad = jnp.sum(dq_parts.astype(F32), axis=0).astype(BF)
    q_other = swap(query_grad, "head")
    kv_grad = jnp.sum(dkv_parts.astype(F32), axis=0).astype(BF)
    kv_other = swap(kv_grad, "head")

    ins = [conv_input, x_swapped[0], x_far[0], x_swapped[1], x_far[1], x_swapped[2]]
    g_pair, g_high, filter_part = project_and_filter(
        place, block_order, query_grad, kv_grad, q_other, kv_other, qkv_weight, w_other, ins
    )

    mine_sum = filter_part[0] + swap(filter_part[1], "core")
    far = [from_ctx(g_pair, 2), from_ctx(g_high, -2)]
    g_partner = swap(g_pair, "core")
    parts = lax.all_to_all(
        mine_sum.reshape(chips, channels // 2 // chips, TAPS), ("xl", "y", "z"), 0, 0, tiled=True
    )
    parts, far, g_partner = lax.optimization_barrier((parts, far, g_partner))
    total = jnp.sum(parts, axis=0)
    total, far = lax.optimization_barrier((total, far))
    grads = [g_pair, g_partner, far[0], swap(far[0], "core"), far[1], swap(far[1], "core")]
    half = to_all(total, ("xl", "y", "z"), chips)
    input_grad = input_conv(place, block_order, grads, conv_filter)
    half, input_grad = lax.optimization_barrier((half, input_grad))
    half = half.reshape(channels // 2, TAPS)
    other = swap(half, "core")
    filter_grad = jnp.concatenate(
        (jnp.where(core == 0, half, other), jnp.where(core == 0, other, half)), axis=0
    )
    return input_grad, filter_grad


def solution(mesh):
    fine = Mesh(mesh.devices.reshape(XL, Y, Z, CORE, HEAD), CTX + ("head",))
    rows = P(CTX, "head")
    return jax.shard_map(
        local,
        mesh=fine,
        in_specs=(P(), rows, P("head", None), rows, rows, rows, rows, P(None, None, "head")),
        out_specs=(rows, P("head", None)),
        check_vma=False,
    )
```
